32 devices in a mesh: sec: 4 (over y, x), blk: 8 (over z, core).
Axes of the slice: x: 2, y: 2, z: 4, core: 2. Of those that a mesh axis runs over, the one named last changes fastest.
Arguments:
- velocity: bfloat16 [16, 3, 64, 512], P(None, None, ('sec', 'blk')), may hold values from -6 to 6
- geometry: float32 [9, 64, 512], P(None, ('sec', 'blk')), may hold values from -4 to 4
- mass: float32 [64, 512], P(('sec', 'blk')), may hold values from 0.5 to 2
- snapshots: bfloat16 [512, 3, 64, 512], P(None, None, ('sec', 'blk')), may hold values from -6 to 6
- eigvecs: float32 [512, 256], P('blk'), may hold values from -0.25 to 0.25
- mode_order: int32 [256], replicated, may hold values from 0 to 255, each once
- elem_map: int32 [64], P(('sec', 'blk')), may hold values from 0 to 1, as said below
Outputs:
- coefficients: float32 [16, 256], P('sec', 'blk')
The draws below stay inside these ranges and needn't reach their ends.
Inputs may be any that keep to these rules, and one draw needn't show every extreme that they name: `elem_map`: each aligned run of 2 entries (the elements of one device) holds each of 0 to 1 once. `mode_order`: A permutation of the modes.
All inputs are finite; a program needn't handle non-finite values.
Results may differ from the reference program's by a relative error of at most 0.0075.
Values sent between devices are 32-bit elements; how exact they have to be, the bound alone decides.
No kernel may reach another device: no remote copies, remote signals or barrier semaphores. Data moves between devices by JAX's collectives and lax.ppermute only.
A program may use at most 64 MiB of HBM per device.

```python
import math
import jax
import jax.numpy as jnp
import numpy as np
from jax import lax

PTS = 512
MODES = 256
M = 512
E_DEV = 2
FIELDS = 16
ELEMS = 64


def block_permutation(key):
    return jax.random.permutation(key, E_DEV)


def draw_elem_map(key, part):
    groups = ELEMS // E_DEV
    keys = jax.random.split(jax.random.fold_in(key, 11), groups)
    perms = jax.vmap(block_permutation)(keys)
    return perms.reshape(ELEMS).astype(jnp.int32)


def levels(stream_key, extent, pieces, least, high):
    factor_of, own = 1.0, jax.random.fold_in(stream_key, 6)
    for dim, parts in pieces:
        steps = jnp.exp(jax.random.uniform(jax.random.fold_in(own, dim), (parts,), jnp.float32, least / len(pieces), high / len(pieces)))
        factor_of = factor_of * jnp.repeat(steps, extent[dim] // parts).reshape([-1 if axis == dim else 1 for axis in range(len(extent))])
    return factor_of


def gaussian(rng, dims, spread, most, cuts=(), held_as=jnp.bfloat16):
    values = spread * jax.random.normal(rng, dims, jnp.float32)
    if cuts:
        values = values * levels(rng, dims, cuts, -0.22, 0.18)
    return jnp.clip(values, -most, most).astype(held_as)


def setup_inputs(seed: int = 0) -> dict:
    streams_of = jax.random.split(jax.random.key(seed), 8)
    velocity = gaussian(streams_of[0], (FIELDS, 3, ELEMS, PTS), 1.0, 6.0, ((2, 32),))
    geometry = gaussian(streams_of[1], (9, ELEMS, PTS), 0.3, 4.0, ((1, 32),), jnp.float32)
    mass = jnp.clip(jnp.exp(math.log(2.0) - 1.3862944 * jax.random.uniform(streams_of[2], (ELEMS, PTS), jnp.float32) ** levels(streams_of[2], (ELEMS, PTS), ((0, 32),), -0.2, 0.2)), 0.5, 2.0)
    snapshots = gaussian(streams_of[3], (M, 3, ELEMS, PTS), 1.0, 6.0, ((2, 32),))
    eigvecs = gaussian(streams_of[4], (M, MODES), M ** -0.5, 0.25, ((0, 8),), jnp.float32)
    mode_order = jax.random.permutation(streams_of[5], MODES).astype(jnp.int32)
    elem_map = draw_elem_map(jax.random.fold_in(streams_of[7], 71), 0)
    return {"velocity": velocity, "geometry": geometry, "mass": mass, "snapshots": snapshots, "eigvecs": eigvecs, "mode_order": mode_order, "elem_map": elem_map}


GLL_NODES = np.array([-1.0, -0.8717401485096066, -0.5917001814331423, -0.2092992179024789, 0.2092992179024789, 0.5917001814331423, 0.8717401485096066, 1.0])
GLL_WEIGHTS = np.array([1.0 / 28.0, 0.2107042271435061, 0.3411226924835044, 0.4124587946587038, 0.4124587946587038, 0.3411226924835044, 0.2107042271435061, 1.0 / 28.0])

def legendre_seven(nodes):
    before = nodes * 0.0 + 1.0
    current = nodes * 1.0
    for order in range(1, 7):
        following = ((2.0 * order + 1.0) * nodes * current - order * before) / (order + 1.0)
        before = current
        current = following
    return current

def derivative_matrix():
    degree = 7
    values = legendre_seven(GLL_NODES)
    result = np.zeros((8, 8))
    for row_idx in range(8):
        for col_idx in range(8):
            if row_idx != col_idx:
                result[row_idx, col_idx] = values[row_idx] / (values[col_idx] * (GLL_NODES[row_idx] - GLL_NODES[col_idx]))
    result[0, 0] = -degree * (degree + 1) / 4.0
    result[7, 7] = degree * (degree + 1) / 4.0
    return result

def point_weights():
    cube = GLL_WEIGHTS[:, None, None] * GLL_WEIGHTS[None, :, None] * GLL_WEIGHTS[None, None, :]
    return cube.reshape(512)

def reference(velocity, geometry, mass, snapshots, eigvecs, mode_order, elem_map):
    table = jnp.asarray(derivative_matrix(), jnp.float32)
    weight_cube = jnp.asarray(point_weights(), jnp.float32)
    highest = lax.Precision.HIGHEST
    groups = ELEMS // E_DEV

    def step(carry, group):
        start = (group * E_DEV).astype(jnp.int32)
        velocity_block = lax.dynamic_slice_in_dim(velocity, start, E_DEV, 2)
        geometry_block = lax.dynamic_slice_in_dim(geometry, start, E_DEV, 1)
        mass_block = lax.dynamic_slice_in_dim(mass, start, E_DEV, 0)
        snapshot_block = lax.dynamic_slice_in_dim(snapshots, start, E_DEV, 2)
        map_block = lax.dynamic_slice_in_dim(elem_map, start, E_DEV, 0).astype(jnp.int32)
        cube = velocity_block.astype(jnp.float32).reshape(FIELDS, 3, E_DEV, 8, 8, 8)
        along_r = jnp.einsum('ai,scdijk->scdajk', table, cube, precision=highest).reshape(FIELDS, 3, E_DEV, PTS)
        along_s = jnp.einsum('aj,scdijk->scdiak', table, cube, precision=highest).reshape(FIELDS, 3, E_DEV, PTS)
        along_t = jnp.einsum('ak,scdijk->scdija', table, cube, precision=highest).reshape(FIELDS, 3, E_DEV, PTS)

        def gradient(component, coord):
            return geometry_block[coord] * along_r[:, component] + geometry_block[3 + coord] * along_s[:, component] + geometry_block[6 + coord] * along_t[:, component]
        vorticity = jnp.stack([gradient(2, 1) - gradient(1, 2), gradient(0, 2) - gradient(2, 0), gradient(1, 0) - gradient(0, 1)], axis=1)
        weighted = (mass_block * weight_cube * vorticity).astype(jnp.bfloat16)
        chosen = jnp.take(snapshot_block, map_block, axis=2)
        update = jnp.dot(weighted.reshape(FIELDS, 3 * E_DEV * PTS), chosen.reshape(M, 3 * E_DEV * PTS).T, preferred_element_type=jnp.float32)
        return (carry + update, None)
    init = jnp.zeros((FIELDS, M), jnp.float32)
    contracted, _ = lax.scan(step, init, jnp.arange(groups, dtype=jnp.int32))
    ordered = eigvecs[:, mode_order]
    return jnp.dot(contracted, ordered, precision=highest) * (0.25 / math.sqrt(ELEMS))
```

```python
import math

import jax
import jax.numpy as jnp
import numpy as np
from jax import lax
from jax.sharding import PartitionSpec as P

GLL_NODES = np.array(
    [
        -1.0,
        -0.8717401485096066,
        -0.5917001814331423,
        -0.2092992179024789,
        0.2092992179024789,
        0.5917001814331423,
        0.8717401485096066,
        1.0,
    ]
)
GLL_WEIGHTS = np.array(
    [
        1.0 / 28.0,
        0.2107042271435061,
        0.3411226924835044,
        0.4124587946587038,
        0.4124587946587038,
        0.3411226924835044,
        0.2107042271435061,
        1.0 / 28.0,
    ]
)


def legendre_seven(nodes):
    before = nodes * 0.0 + 1.0
    current = nodes * 1.0
    for order in range(1, 7):
        following = ((2.0 * order + 1.0) * nodes * current - order * before) / (order + 1.0)
        before = current
        current = following
    return current


def derivative_matrix():
    degree = 7
    values = legendre_seven(GLL_NODES)
    result = np.zeros((8, 8))
    for row_idx in range(8):
        for col_idx in range(8):
            if row_idx != col_idx:
                result[row_idx, col_idx] = values[row_idx] / (
                    values[col_idx] * (GLL_NODES[row_idx] - GLL_NODES[col_idx])
                )
    result[0, 0] = -degree * (degree + 1) / 4.0
    result[7, 7] = degree * (degree + 1) / 4.0
    return result.astype(np.float32)


def point_weights():
    cube = GLL_WEIGHTS[:, None, None] * GLL_WEIGHTS[None, :, None] * GLL_WEIGHTS[None, None, :]
    return cube.reshape(512).astype(np.float32)


def vorticity_weighted(velocity, geometry, mass):
    fields, components, elements, points = velocity.shape
    highest = lax.Precision.HIGHEST
    table = jnp.asarray(derivative_matrix())
    cube = velocity.astype(jnp.float32).reshape(fields, components, elements, 8, 8, 8)
    along_r = jnp.einsum("ai,scdijk->scdajk", table, cube, precision=highest).reshape(
        fields, components, elements, points
    )
    along_s = jnp.einsum("aj,scdijk->scdiak", table, cube, precision=highest).reshape(
        fields, components, elements, points
    )
    along_t = jnp.einsum("ak,scdijk->scdija", table, cube, precision=highest).reshape(
        fields, components, elements, points
    )

    def gradient(component, coord):
        return (
            geometry[coord] * along_r[:, component]
            + geometry[3 + coord] * along_s[:, component]
            + geometry[6 + coord] * along_t[:, component]
        )

    vorticity = jnp.stack(
        [
            gradient(2, 1) - gradient(1, 2),
            gradient(0, 2) - gradient(2, 0),
            gradient(1, 0) - gradient(0, 1),
        ],
        axis=1,
    )
    return (mass * jnp.asarray(point_weights()) * vorticity).astype(jnp.bfloat16)


def exchange(block, ds, db):
    sections, blocks = lax.axis_size("sec"), lax.axis_size("blk")
    pairs = [
        (s * blocks + b, (s ^ ds) * blocks + (b ^ db))
        for s in range(sections)
        for b in range(blocks)
    ]
    return lax.ppermute(block, ("sec", "blk"), pairs)


def reduced_sums(partial):
    sections, blocks = lax.axis_size("sec"), lax.axis_size("blk")
    section = lax.axis_index("sec")
    sums = partial + exchange(partial, 0, 1)
    step = sections // 2
    while step:
        half = sums.shape[0] // 2
        low, high = sums[:half], sums[half:]
        upper = (section & step) != 0
        sums = jnp.where(upper, high, low) + exchange(jnp.where(upper, low, high), step, 1)
        step //= 2
    step = 2
    while step < blocks:
        sums = sums + exchange(sums, 0, step | 1)
        step *= 2
    return sums


def own_columns(eigvecs, mode_order):
    blocks = lax.axis_size("blk")
    block = lax.axis_index("blk")
    mode_count = mode_order.shape[0]
    cols = mode_count // blocks
    relative = []
    for place in range(blocks):
        core, chip = place // (blocks // 2), place % (blocks // 2)
        odd = bin(chip).count("1") & 1
        relative.append(2 * chip + (core ^ odd))
    wanted = jnp.take(
        mode_order.reshape(blocks, cols), block ^ jnp.asarray(relative, jnp.int32), axis=0
    ).reshape(mode_count)
    selector = (
        wanted[:, None] == lax.broadcasted_iota(jnp.int32, (mode_count, mode_count), 1)
    ).astype(jnp.float32)
    table = lax.dot_general(
        selector, eigvecs, (((1,), (1,)), ((), ())), precision=lax.Precision.HIGHEST
    )
    half = mode_count // 2
    keep, got = table[:half], exchange(table[half:], 0, 1)
    odd = (block & 1) != 0
    held = [
        jnp.concatenate([jnp.where(odd, got, keep), jnp.where(odd, keep, got)], axis=1)
    ]
    step = blocks // 2
    while step > 1:
        half = held[0].shape[0] // 2
        send = jnp.concatenate([part[half:] for part in held], axis=0)
        got = exchange(send, 0, step | 1)
        held = [part[:half] for part in held] + [
            got[i * half : (i + 1) * half] for i in range(len(held))
        ]
        step //= 2
    return held


def pair_order():
    blocks = lax.axis_size("blk")
    order = [0]
    step = blocks // 2
    while step > 1:
        order += [other ^ step for other in order]
        step //= 2
    return [other // 2 for other in order]


def shards(velocity, geometry, mass, snapshots, eigvecs, mode_order, elem_map):
    highest = lax.Precision.HIGHEST
    weighted = vorticity_weighted(velocity, geometry, mass)
    fields, components, elements, points = weighted.shape
    slot_index = lax.broadcasted_iota(jnp.int32, (elements, elements), 0)
    onehot = (slot_index == elem_map[None, :]).astype(jnp.bfloat16)
    stored = jnp.einsum(
        "fe,scep->scfp", onehot, weighted, preferred_element_type=jnp.float32
    ).astype(jnp.bfloat16)
    stored_flat = stored.reshape(fields, components * elements * points)
    snap_flat = snapshots.reshape(snapshots.shape[0], components * elements * points)
    factor = 0.25 / math.sqrt(elements * lax.axis_size("sec") * lax.axis_size("blk"))
    contracted = lax.dot_general(
        stored_flat, snap_flat, (((1,), (1,)), ((), ())), preferred_element_type=jnp.float32
    )
    columns = own_columns(eigvecs, mode_order)
    sums = reduced_sums(contracted)
    chips = lax.axis_size("blk") // 2
    chip = lax.axis_index("blk") // 2
    parts = jnp.take(
        sums.reshape(sums.shape[0], chips, sums.shape[1] // chips),
        chip ^ jnp.asarray(pair_order(), jnp.int32),
        axis=1,
    ).reshape(sums.shape)
    share = lax.dot_general(
        parts, jnp.concatenate(columns, axis=1), (((1,), (1,)), ((), ())), precision=highest
    )
    return share * factor


def solution(mesh):
    placed = (
        P(None, None, ("sec", "blk"), None),
        P(None, ("sec", "blk"), None),
        P(("sec", "blk"), None),
        P(None, None, ("sec", "blk"), None),
        P("blk", None),
        P(),
        P(("sec", "blk")),
    )
    return jax.shard_map(
        shards, mesh=mesh, in_specs=placed, out_specs=P("sec", "blk"), check_vma=False
    )
```

```python
import math

import jax
import jax.numpy as jnp
import ml_dtypes
import numpy as np
from jax import lax
from jax.experimental import pallas as pl
from jax.experimental.pallas import tpu as pltpu
from jax.sharding import PartitionSpec as P

LANES = 128

GLL_NODES = np.array(
    [
        -1.0,
        -0.8717401485096066,
        -0.5917001814331423,
        -0.2092992179024789,
        0.2092992179024789,
        0.5917001814331423,
        0.8717401485096066,
        1.0,
    ]
)
GLL_WEIGHTS = np.array(
    [
        1.0 / 28.0,
        0.2107042271435061,
        0.3411226924835044,
        0.4124587946587038,
        0.4124587946587038,
        0.3411226924835044,
        0.2107042271435061,
        1.0 / 28.0,
    ]
)


def legendre_seven(nodes):
    before = nodes * 0.0 + 1.0
    current = nodes * 1.0
    for order in range(1, 7):
        following = ((2.0 * order + 1.0) * nodes * current - order * before) / (order + 1.0)
        before = current
        current = following
    return current


def derivative_matrix():
    degree = 7
    values = legendre_seven(GLL_NODES)
    result = np.zeros((8, 8))
    for row_idx in range(8):
        for col_idx in range(8):
            if row_idx != col_idx:
                result[row_idx, col_idx] = values[row_idx] / (
                    values[col_idx] * (GLL_NODES[row_idx] - GLL_NODES[col_idx])
                )
    result[0, 0] = -degree * (degree + 1) / 4.0
    result[7, 7] = degree * (degree + 1) / 4.0
    return result.astype(np.float32)


def point_weights():
    cube = GLL_WEIGHTS[:, None, None] * GLL_WEIGHTS[None, :, None] * GLL_WEIGHTS[None, None, :]
    return cube.reshape(512).astype(np.float32)


def along_tables(points):
    table = derivative_matrix()
    side = table.shape[0]
    lanes = np.arange(LANES)
    per_block = LANES // (side * side)
    r_rows = np.zeros((points // LANES * side, LANES), np.float32)
    for block in range(points // LANES):
        for node in range(side):
            r_rows[block * side + node] = table[block * per_block + lanes // (side * side), node]
    i, j, k = lanes // (side * side), lanes // side % side, lanes % side
    along_s = table[j[None, :], j[:, None]] * (i[None, :] == i[:, None]) * (k[None, :] == k[:, None])
    along_t = table[k[None, :], k[:, None]] * (i[None, :] == i[:, None]) * (j[None, :] == j[:, None])
    both = np.concatenate([along_s, along_t], axis=1).astype(np.float32)
    high = both.astype(ml_dtypes.bfloat16)
    low = (both - high.astype(np.float32)).astype(ml_dtypes.bfloat16)
    return r_rows, np.concatenate([high, low], axis=0)


def vorticity_kernel(map_ref, velocity_ref, geometry_ref, mass_ref, point_ref, r_ref, st_ref, out_ref):
    components, elements, fields, points = velocity_ref.shape
    blocks = points // LANES
    side = r_ref.shape[0] // blocks
    lane = lax.broadcasted_iota(jnp.int32, (fields, LANES), 1)
    lower = lane < LANES // 2
    for elem in range(elements):
        packed = [
            [velocity_ref[c, elem, :, b * LANES : (b + 1) * LANES] for b in range(blocks)]
            for c in range(components)
        ]
        stacked = jnp.concatenate([packed[c][b] for c in range(components) for b in range(blocks)], axis=0)
        along_st = jnp.dot(
            jnp.concatenate([stacked, stacked], axis=1), st_ref[...], preferred_element_type=jnp.float32
        )
        along_r = []
        for c in range(components):
            nodes = []
            for b in range(blocks):
                own = packed[c][b].astype(jnp.float32)
                other = pltpu.roll(own, LANES // 2, 1)
                nodes += [jnp.where(lower, own, other), jnp.where(lower, other, own)]
            for b in range(blocks):
                total = r_ref[b * side : b * side + 1, :] * nodes[0]
                for node in range(1, side):
                    total += r_ref[b * side + node : b * side + node + 1, :] * nodes[node]
                along_r.append(total)
        slot = map_ref[elem]
        for b in range(blocks):
            lanes = slice(b * LANES, (b + 1) * LANES)
            weight = mass_ref[elem : elem + 1, lanes] * point_ref[:, lanes]
            factors = [weight * geometry_ref[n, elem : elem + 1, lanes] for n in range(9)]

            def gradient(component, coord):
                row = (component * blocks + b) * fields
                part = along_st[row : row + fields]
                return (
                    factors[coord] * along_r[component * blocks + b]
                    + factors[3 + coord] * part[:, :LANES]
                    + factors[6 + coord] * part[:, LANES:]
                )

            for c in range(components):
                after, last = (c + 1) % 3, (c + 2) % 3
                out_ref[c, slot, :, lanes] = (gradient(last, after) - gradient(after, last)).astype(jnp.bfloat16)


def stored_vorticity(velocity, geometry, mass, elem_map):
    fields, components, elements, points = velocity.shape
    r_rows, st = along_tables(points)
    vmem = pl.BlockSpec(memory_space=pltpu.VMEM)
    return pl.pallas_call(
        vorticity_kernel,
        out_shape=jax.ShapeDtypeStruct((components, elements, fields, points), jnp.bfloat16),
        in_specs=[pl.BlockSpec(memory_space=pltpu.SMEM)] + [vmem] * 6,
        out_specs=vmem,
    )(
        elem_map,
        velocity.transpose(1, 2, 0, 3),
        geometry,
        mass,
        jnp.asarray(point_weights()).reshape(1, points),
        jnp.asarray(r_rows),
        jnp.asarray(st),
    )


def exchange(block, ds, db):
    sections, blocks = lax.axis_size("sec"), lax.axis_size("blk")
    pairs = [
        (s * blocks + b, (s ^ ds) * blocks + (b ^ db))
        for s in range(sections)
        for b in range(blocks)
    ]
    return lax.ppermute(block, ("sec", "blk"), pairs)


def reduced_sums(partial):
    sections, blocks = lax.axis_size("sec"), lax.axis_size("blk")
    section = lax.axis_index("sec")
    sums = partial + exchange(partial, 0, 1)
    step = sections // 2
    while step:
        half = sums.shape[0] // 2
        low, high = sums[:half], sums[half:]
        upper = (section & step) != 0
        sums = jnp.where(upper, high, low) + exchange(jnp.where(upper, low, high), step, 1)
        step //= 2
    step = 2
    while step < blocks:
        sums = sums + exchange(sums, 0, step | 1)
        step *= 2
    return sums


def own_columns(eigvecs, mode_order):
    blocks = lax.axis_size("blk")
    block = lax.axis_index("blk")
    mode_count = mode_order.shape[0]
    cols = mode_count // blocks
    relative = []
    for place in range(blocks):
        core, chip = place // (blocks // 2), place % (blocks // 2)
        odd = bin(chip).count("1") & 1
        relative.append(2 * chip + (core ^ odd))
    wanted = jnp.take(
        mode_order.reshape(blocks, cols), block ^ jnp.asarray(relative, jnp.int32), axis=0
    ).reshape(mode_count)
    selector = (
        wanted[:, None] == lax.broadcasted_iota(jnp.int32, (mode_count, mode_count), 1)
    ).astype(jnp.float32)
    table = lax.dot_general(
        selector, eigvecs, (((1,), (1,)), ((), ())), precision=lax.Precision.HIGHEST
    )
    half = mode_count // 2
    keep, got = table[:half], exchange(table[half:], 0, 1)
    odd = (block & 1) != 0
    held = [
        jnp.concatenate([jnp.where(odd, got, keep), jnp.where(odd, keep, got)], axis=1)
    ]
    step = blocks // 2
    while step > 1:
        half = held[0].shape[0] // 2
        send = jnp.concatenate([part[half:] for part in held], axis=0)
        got = exchange(send, 0, step | 1)
        held = [part[:half] for part in held] + [
            got[i * half : (i + 1) * half] for i in range(len(held))
        ]
        step //= 2
    return held


def pair_order():
    blocks = lax.axis_size("blk")
    order = [0]
    step = blocks // 2
    while step > 1:
        order += [other ^ step for other in order]
        step //= 2
    return [other // 2 for other in order]


def shards(velocity, geometry, mass, snapshots, eigvecs, mode_order, elem_map):
    highest = lax.Precision.HIGHEST
    stored = stored_vorticity(velocity, geometry, mass, elem_map)
    components, elements, fields, points = stored.shape
    factor = 0.25 / math.sqrt(elements * lax.axis_size("sec") * lax.axis_size("blk"))
    contracted = lax.dot_general(
        stored,
        snapshots,
        (((0, 1, 3), (1, 2, 3)), ((), ())),
        preferred_element_type=jnp.float32,
    )
    columns = own_columns(eigvecs, mode_order)
    sums = reduced_sums(contracted)
    chips = lax.axis_size("blk") // 2
    chip = lax.axis_index("blk") // 2
    parts = jnp.take(
        sums.reshape(sums.shape[0], chips, sums.shape[1] // chips),
        chip ^ jnp.asarray(pair_order(), jnp.int32),
        axis=1,
    ).reshape(sums.shape)
    share = lax.dot_general(
        parts, jnp.concatenate(columns, axis=1), (((1,), (1,)), ((), ())), precision=highest
    )
    return share * factor


def solution(mesh):
    placed = (
        P(None, None, ("sec", "blk"), None),
        P(None, ("sec", "blk"), None),
        P(("sec", "blk"), None),
        P(None, None, ("sec", "blk"), None),
        P("blk", None),
        P(),
        P(("sec", "blk")),
    )
    return jax.shard_map(
        shards, mesh=mesh, in_specs=placed, out_specs=P("sec", "blk"), check_vma=False
    )
```

```python
import math

import jax
import jax.numpy as jnp
import ml_dtypes
import numpy as np
from jax import lax
from jax.experimental import pallas as pl
from jax.experimental.pallas import tpu as pltpu
from jax.sharding import PartitionSpec as P

LANES = 128

GLL_NODES = np.array(
    [
        -1.0,
        -0.8717401485096066,
        -0.5917001814331423,
        -0.2092992179024789,
        0.2092992179024789,
        0.5917001814331423,
        0.8717401485096066,
        1.0,
    ]
)
GLL_WEIGHTS = np.array(
    [
        1.0 / 28.0,
        0.2107042271435061,
        0.3411226924835044,
        0.4124587946587038,
        0.4124587946587038,
        0.3411226924835044,
        0.2107042271435061,
        1.0 / 28.0,
    ]
)


def legendre_seven(nodes):
    before = nodes * 0.0 + 1.0
    current = nodes * 1.0
    for order in range(1, 7):
        following = ((2.0 * order + 1.0) * nodes * current - order * before) / (order + 1.0)
        before = current
        current = following
    return current


def derivative_matrix():
    degree = 7
    values = legendre_seven(GLL_NODES)
    result = np.zeros((8, 8))
    for row_idx in range(8):
        for col_idx in range(8):
            if row_idx != col_idx:
                result[row_idx, col_idx] = values[row_idx] / (
                    values[col_idx] * (GLL_NODES[row_idx] - GLL_NODES[col_idx])
                )
    result[0, 0] = -degree * (degree + 1) / 4.0
    result[7, 7] = degree * (degree + 1) / 4.0
    return result.astype(np.float32)


def point_weights():
    cube = GLL_WEIGHTS[:, None, None] * GLL_WEIGHTS[None, :, None] * GLL_WEIGHTS[None, None, :]
    return cube.reshape(512).astype(np.float32)


def along_tables(points):
    table = derivative_matrix()
    side = table.shape[0]
    lanes = np.arange(LANES)
    per_block = LANES // (side * side)
    r_rows = np.zeros((points // LANES * side, LANES), np.float32)
    for block in range(points // LANES):
        for node in range(side):
            r_rows[block * side + node] = table[block * per_block + lanes // (side * side), node]
    i, j, k = lanes // (side * side), lanes // side % side, lanes % side
    along_s = table[j[None, :], j[:, None]] * (i[None, :] == i[:, None]) * (k[None, :] == k[:, None])
    along_t = table[k[None, :], k[:, None]] * (i[None, :] == i[:, None]) * (j[None, :] == j[:, None])
    both = np.concatenate([along_s, along_t], axis=1).astype(np.float32)
    high = both.astype(ml_dtypes.bfloat16)
    low = (both - high.astype(np.float32)).astype(ml_dtypes.bfloat16)
    return r_rows, np.concatenate([high, low], axis=0)


def pair_rows(rows, height):
    elements = rows.shape[0]
    turn = lax.broadcasted_iota(jnp.int32, (height, LANES), 0) % elements
    spread = jnp.broadcast_to(rows[0:1], (height, LANES))
    for elem in range(1, elements):
        spread = jnp.where(turn == elem, rows[elem : elem + 1], spread)
    return spread


def partial_kernel(
    map_ref,
    velocity_hbm,
    geometry_hbm,
    mass_hbm,
    point_hbm,
    r_hbm,
    st_hbm,
    snapshots_hbm,
    out_ref,
    velocity_ref,
    geometry_ref,
    mass_ref,
    point_ref,
    r_ref,
    st_ref,
    snapshots_ref,
    product_ref,
    turned_ref,
    semaphores,
):
    fields, components, elements, points = velocity_hbm.shape
    snaps = snapshots_hbm.shape[0]
    blocks = points // LANES
    side = r_hbm.shape[0] // blocks
    rows = fields * elements
    chunks = [(c, b) for c in range(components) for b in range(blocks)]
    small = [
        (geometry_hbm, geometry_ref),
        (mass_hbm, mass_ref),
        (point_hbm, point_ref),
        (r_hbm, r_ref),
        (st_hbm, st_ref),
    ]
    for n, (c, b) in enumerate(chunks):
        small.append((velocity_hbm.at[:, c, :, pl.ds(b * LANES, LANES)], velocity_ref.at[n]))
    large = [
        (snapshots_hbm.at[:, c, :, pl.ds(b * LANES, LANES)], snapshots_ref.at[n])
        for n, (c, b) in enumerate(chunks)
    ]
    copies = [
        pltpu.make_async_copy(source, target, semaphores.at[n])
        for n, (source, target) in enumerate(small + large)
    ]
    for copy in copies:
        copy.start()
    for copy in copies[: len(small)]:
        copy.wait()

    packed = [velocity_ref.at[n].reshape(rows, LANES)[...] for n in range(len(chunks))]
    stacked = jnp.concatenate(packed, axis=0)
    along_st = jnp.dot(
        jnp.concatenate([stacked, stacked], axis=1), st_ref[...], preferred_element_type=jnp.float32
    )
    lower = lax.broadcasted_iota(jnp.int32, (rows, LANES), 1) < LANES // 2
    along_r = []
    for c in range(components):
        nodes = []
        for b in range(blocks):
            own = packed[c * blocks + b].astype(jnp.float32)
            other = pltpu.roll(own, LANES // 2, 1)
            nodes += [jnp.where(lower, own, other), jnp.where(lower, other, own)]
        for b in range(blocks):
            total = r_ref[b * side : b * side + 1, :] * nodes[0]
            for node in range(1, side):
                total += r_ref[b * side + node : b * side + node + 1, :] * nodes[node]
            along_r.append(total)

    weighted = [None] * len(chunks)
    for b in range(blocks):
        lanes = slice(b * LANES, (b + 1) * LANES)
        weight = mass_ref[:, lanes] * point_ref[:, lanes]
        factors = [pair_rows(weight * geometry_ref[n, :, lanes], rows) for n in range(9)]

        def gradient(component, coord):
            row = (component * blocks + b) * rows
            part = along_st[row : row + rows]
            return (
                factors[coord] * along_r[component * blocks + b]
                + factors[3 + coord] * part[:, :LANES]
                + factors[6 + coord] * part[:, LANES:]
            )

        for c in range(components):
            after, last = (c + 1) % 3, (c + 2) % 3
            weighted[c * blocks + b] = (gradient(last, after) - gradient(after, last)).astype(jnp.bfloat16)
    weighted = jnp.concatenate(weighted, axis=1)

    for copy in copies[len(small) :]:
        copy.wait()
    height = snaps * elements
    step = min(height, 256)
    for start in range(0, height, step):
        part = jnp.concatenate(
            [snapshots_ref.at[n].reshape(height, LANES)[start : start + step] for n in range(len(chunks))], axis=1
        )
        product_ref[start : start + step, :rows] = lax.dot_general(
            part, weighted, (((1,), (1,)), ((), ())), preferred_element_type=jnp.float32
        )
    turn = lax.broadcasted_iota(jnp.int32, (snaps, rows), 1) % elements
    chosen = jnp.zeros((snaps, rows), jnp.float32)
    for slot in range(elements):
        here = product_ref[pl.ds(slot, snaps, stride=elements), :][:, :rows]
        for elem in range(elements):
            chosen = jnp.where((turn == elem) & (map_ref[elem] == slot), here, chosen)
    for n in range(snaps // LANES):
        turned_ref[n * rows : (n + 1) * rows, :] = chosen[n * LANES : (n + 1) * LANES, :].T
    for n in range(snaps // LANES):
        total = turned_ref[pl.ds(n * rows, fields, stride=elements), :]
        for elem in range(1, elements):
            total += turned_ref[pl.ds(n * rows + elem, fields, stride=elements), :]
        out_ref[:, n * LANES : (n + 1) * LANES] = total


def partial_sums(velocity, geometry, mass, snapshots, elem_map):
    fields, components, elements, points = velocity.shape
    snaps = snapshots.shape[0]
    r_rows, st = along_tables(points)
    chunks = components * (points // LANES)
    rows = fields * elements
    anywhere = pl.BlockSpec(memory_space=pltpu.HBM)
    return pl.pallas_call(
        partial_kernel,
        out_shape=jax.ShapeDtypeStruct((fields, snaps), jnp.float32),
        in_specs=[pl.BlockSpec(memory_space=pltpu.SMEM)] + [anywhere] * 7,
        out_specs=pl.BlockSpec(memory_space=pltpu.VMEM),
        scratch_shapes=[
            pltpu.VMEM((chunks, fields, elements, LANES), jnp.bfloat16),
            pltpu.VMEM(geometry.shape, jnp.float32),
            pltpu.VMEM(mass.shape, jnp.float32),
            pltpu.VMEM((1, points), jnp.float32),
            pltpu.VMEM(r_rows.shape, jnp.float32),
            pltpu.VMEM(st.shape, jnp.bfloat16),
            pltpu.VMEM((chunks, snaps, elements, LANES), jnp.bfloat16),
            pltpu.VMEM((snaps * elements, LANES), jnp.float32),
            pltpu.VMEM((snaps // LANES * rows, LANES), jnp.float32),
            pltpu.SemaphoreType.DMA((5 + 2 * chunks,)),
        ],
        compiler_params=pltpu.CompilerParams(vmem_limit_bytes=40 * 1024 * 1024),
    )(
        elem_map,
        *[
            pltpu.with_memory_space_constraint(array, pltpu.HBM)
            for array in (
                velocity,
                geometry,
                mass,
                jnp.asarray(point_weights()).reshape(1, points),
                jnp.asarray(r_rows),
                jnp.asarray(st),
                snapshots,
            )
        ],
    )


def exchange(block, ds, db):
    sections, blocks = lax.axis_size("sec"), lax.axis_size("blk")
    pairs = [
        (s * blocks + b, (s ^ ds) * blocks + (b ^ db))
        for s in range(sections)
        for b in range(blocks)
    ]
    return lax.ppermute(block, ("sec", "blk"), pairs)


def reduced_sums(partial):
    sections, blocks = lax.axis_size("sec"), lax.axis_size("blk")
    section = lax.axis_index("sec")
    sums = partial + exchange(partial, 0, 1)
    step = sections // 2
    while step:
        half = sums.shape[0] // 2
        low, high = sums[:half], sums[half:]
        upper = (section & step) != 0
        sums = jnp.where(upper, high, low) + exchange(jnp.where(upper, low, high), step, 1)
        step //= 2
    step = 2
    while step < blocks:
        sums = sums + exchange(sums, 0, step | 1)
        step *= 2
    return sums


def own_columns(eigvecs, mode_order):
    blocks = lax.axis_size("blk")
    block = lax.axis_index("blk")
    mode_count = mode_order.shape[0]
    cols = mode_count // blocks
    relative = []
    for place in range(blocks):
        core, chip = place // (blocks // 2), place % (blocks // 2)
        odd = bin(chip).count("1") & 1
        relative.append(2 * chip + (core ^ odd))
    wanted = jnp.take(
        mode_order.reshape(blocks, cols), block ^ jnp.asarray(relative, jnp.int32), axis=0
    ).reshape(mode_count)
    selector = (
        wanted[:, None] == lax.broadcasted_iota(jnp.int32, (mode_count, mode_count), 1)
    ).astype(jnp.float32)
    table = lax.dot_general(
        selector, eigvecs, (((1,), (1,)), ((), ())), precision=lax.Precision.HIGHEST
    )
    half = mode_count // 2
    keep, got = table[:half], exchange(table[half:], 0, 1)
    odd = (block & 1) != 0
    held = [
        jnp.concatenate([jnp.where(odd, got, keep), jnp.where(odd, keep, got)], axis=1)
    ]
    step = blocks // 2
    while step > 1:
        half = held[0].shape[0] // 2
        send = jnp.concatenate([part[half:] for part in held], axis=0)
        got = exchange(send, 0, step | 1)
        held = [part[:half] for part in held] + [
            got[i * half : (i + 1) * half] for i in range(len(held))
        ]
        step //= 2
    return held


def pair_order():
    blocks = lax.axis_size("blk")
    order = [0]
    step = blocks // 2
    while step > 1:
        order += [other ^ step for other in order]
        step //= 2
    return [other // 2 for other in order]


def shards(velocity, geometry, mass, snapshots, eigvecs, mode_order, elem_map):
    highest = lax.Precision.HIGHEST
    elements = velocity.shape[2]
    factor = 0.25 / math.sqrt(elements * lax.axis_size("sec") * lax.axis_size("blk"))
    contracted = partial_sums(velocity, geometry, mass, snapshots, elem_map)
    columns = own_columns(eigvecs, mode_order)
    sums = reduced_sums(contracted)
    chips = lax.axis_size("blk") // 2
    chip = lax.axis_index("blk") // 2
    parts = jnp.take(
        sums.reshape(sums.shape[0], chips, sums.shape[1] // chips),
        chip ^ jnp.asarray(pair_order(), jnp.int32),
        axis=1,
    ).reshape(sums.shape)
    share = lax.dot_general(
        parts, jnp.concatenate(columns, axis=1), (((1,), (1,)), ((), ())), precision=highest
    )
    return share * factor


def solution(mesh):
    placed = (
        P(None, None, ("sec", "blk"), None),
        P(None, ("sec", "blk"), None),
        P(("sec", "blk"), None),
        P(None, None, ("sec", "blk"), None),
        P("blk", None),
        P(),
        P(("sec", "blk")),
    )
    return jax.shard_map(
        shards, mesh=mesh, in_specs=placed, out_specs=P("sec", "blk"), check_vma=False
    )
```

```python
import functools
import math

import jax
import jax.numpy as jnp
import ml_dtypes
import numpy as np
from jax import lax
from jax.experimental import pallas as pl
from jax.experimental.pallas import tpu as pltpu
from jax.sharding import PartitionSpec as P

LANES = 128

GLL_NODES = np.array(
    [
        -1.0,
        -0.8717401485096066,
        -0.5917001814331423,
        -0.2092992179024789,
        0.2092992179024789,
        0.5917001814331423,
        0.8717401485096066,
        1.0,
    ]
)
GLL_WEIGHTS = np.array(
    [
        1.0 / 28.0,
        0.2107042271435061,
        0.3411226924835044,
        0.4124587946587038,
        0.4124587946587038,
        0.3411226924835044,
        0.2107042271435061,
        1.0 / 28.0,
    ]
)


def legendre_seven(nodes):
    before = nodes * 0.0 + 1.0
    current = nodes * 1.0
    for order in range(1, 7):
        following = ((2.0 * order + 1.0) * nodes * current - order * before) / (order + 1.0)
        before = current
        current = following
    return current


def derivative_matrix():
    degree = 7
    values = legendre_seven(GLL_NODES)
    result = np.zeros((8, 8))
    for row_idx in range(8):
        for col_idx in range(8):
            if row_idx != col_idx:
                result[row_idx, col_idx] = values[row_idx] / (
                    values[col_idx] * (GLL_NODES[row_idx] - GLL_NODES[col_idx])
                )
    result[0, 0] = -degree * (degree + 1) / 4.0
    result[7, 7] = degree * (degree + 1) / 4.0
    return result.astype(np.float32)


def point_weights():
    cube = GLL_WEIGHTS[:, None, None] * GLL_WEIGHTS[None, :, None] * GLL_WEIGHTS[None, None, :]
    return cube.reshape(512).astype(np.float32)


def along_tables(points):
    table = derivative_matrix()
    side = table.shape[0]
    lanes = np.arange(LANES)
    per_block = LANES // (side * side)
    r_rows = np.zeros((points // LANES * side, LANES), np.float32)
    for block in range(points // LANES):
        for node in range(side):
            r_rows[block * side + node] = table[block * per_block + lanes // (side * side), node]
    i, j, k = lanes // (side * side), lanes // side % side, lanes % side
    along_s = table[j[None, :], j[:, None]] * (i[None, :] == i[:, None]) * (k[None, :] == k[:, None])
    along_t = table[k[None, :], k[:, None]] * (i[None, :] == i[:, None]) * (j[None, :] == j[:, None])
    both = np.concatenate([along_s, along_t], axis=1).astype(np.float32)
    high = both.astype(ml_dtypes.bfloat16)
    low = (both - high.astype(np.float32)).astype(ml_dtypes.bfloat16)
    return r_rows, np.concatenate([high, low], axis=0)


def pair_rows(rows, height):
    elements = rows.shape[0]
    turn = lax.broadcasted_iota(jnp.int32, (height, LANES), 0) % elements
    spread = jnp.broadcast_to(rows[0:1], (height, LANES))
    for elem in range(1, elements):
        spread = jnp.where(turn == elem, rows[elem : elem + 1], spread)
    return spread


def parity(chip):
    return bin(chip).count("1") & 1


def odd_block(block, blocks):
    odd, rest = block & 1, blocks // 2
    while rest > 1:
        block = block >> 1
        odd = odd ^ (block & 1)
        rest //= 2
    return odd


def partial_kernel(
    blocks,
    map_hbm,
    order_hbm,
    velocity_hbm,
    geometry_hbm,
    mass_hbm,
    point_hbm,
    r_hbm,
    st_hbm,
    eigvecs_hbm,
    snapshots_hbm,
    out_ref,
    keep_ref,
    map_ref,
    order_ref,
    velocity_ref,
    geometry_ref,
    mass_ref,
    point_ref,
    r_ref,
    st_ref,
    eigvecs_ref,
    snapshots_ref,
    product_ref,
    turned_ref,
    columns_ref,
    semaphores,
):
    fields, components, elements, points = velocity_hbm.shape
    snaps = snapshots_hbm.shape[0]
    own, mode_count = eigvecs_hbm.shape
    parts = points // LANES
    side = r_hbm.shape[0] // parts
    rows = fields * elements
    chunks = [(c, p) for c in range(components) for p in range(parts)]
    small = [
        (velocity_hbm.at[:, c, :, pl.ds(p * LANES, LANES)], velocity_ref.at[n])
        for n, (c, p) in enumerate(chunks)
    ]
    small += [
        (st_hbm, st_ref),
        (r_hbm, r_ref),
        (geometry_hbm, geometry_ref),
        (mass_hbm, mass_ref),
        (point_hbm, point_ref),
    ]
    large = [
        (map_hbm, map_ref),
        (order_hbm, order_ref),
        (eigvecs_hbm, eigvecs_ref),
    ]
    large += [
        (snapshots_hbm.at[:, c, :, pl.ds(p * LANES, LANES)], snapshots_ref.at[n])
        for n, (c, p) in enumerate(chunks)
    ]
    copies = [
        pltpu.make_async_copy(source, target, semaphores.at[n])
        for n, (source, target) in enumerate(small + large)
    ]
    for copy in copies:
        copy.start()
    for copy in copies[: len(small)]:
        copy.wait()

    packed = [velocity_ref.at[n].reshape(rows, LANES)[...] for n in range(len(chunks))]
    stacked = jnp.concatenate(packed, axis=0)
    along_st = jnp.dot(
        jnp.concatenate([stacked, stacked], axis=1), st_ref[...], preferred_element_type=jnp.float32
    )
    lower = lax.broadcasted_iota(jnp.int32, (rows, LANES), 1) < LANES // 2
    along_r = []
    for c in range(components):
        nodes = []
        for p in range(parts):
            here = packed[c * parts + p].astype(jnp.float32)
            other = pltpu.roll(here, LANES // 2, 1)
            nodes += [jnp.where(lower, here, other), jnp.where(lower, other, here)]
        for p in range(parts):
            total = r_ref[p * side : p * side + 1, :] * nodes[0]
            for node in range(1, side):
                total += r_ref[p * side + node : p * side + node + 1, :] * nodes[node]
            along_r.append(total)

    weighted = [None] * len(chunks)
    for p in range(parts):
        lanes = slice(p * LANES, (p + 1) * LANES)
        weight = mass_ref[:, lanes] * point_ref[:, lanes]
        factors = [pair_rows(weight * geometry_ref[n, :, lanes], rows) for n in range(9)]

        def gradient(component, coord):
            row = (component * parts + p) * rows
            part = along_st[row : row + rows]
            return (
                factors[coord] * along_r[component * parts + p]
                + factors[3 + coord] * part[:, :LANES]
                + factors[6 + coord] * part[:, LANES:]
            )

        for c in range(components):
            after, last = (c + 1) % 3, (c + 2) % 3
            weighted[c * parts + p] = (gradient(last, after) - gradient(after, last)).astype(jnp.bfloat16)
    weighted = jnp.concatenate(weighted, axis=1)

    for copy in copies[len(small) : len(small) + 3]:
        copy.wait()
    selector = (
        lax.broadcasted_iota(jnp.int32, (mode_count, mode_count), 0) == order_ref[...]
    ).astype(jnp.bfloat16)
    rest = eigvecs_ref[...]
    ordered = jnp.zeros(rest.shape, jnp.float32)
    for _ in range(3):
        piece = rest.astype(jnp.bfloat16)
        ordered += jnp.dot(piece, selector, preferred_element_type=jnp.float32)
        rest = rest - piece.astype(jnp.float32)
    columns_ref[...] = ordered.T
    cols, chips = mode_count // blocks, blocks // 2
    odd = odd_block(lax.axis_index("blk"), blocks)
    half = mode_count // 4
    first = fields * chips
    for chip in range(chips):
        even = parity(chip)
        keep = columns_ref[pl.ds((2 * chip + (even ^ odd)) * cols, cols), :]
        send = columns_ref[pl.ds((2 * chip + (even ^ 1 ^ odd)) * cols, cols), :]
        keep_ref[chip * cols : (chip + 1) * cols, :] = keep
        row, lane = chip * cols % half, chip * cols // half * own
        out_ref[first + row : first + row + cols, lane : lane + own] = send

    for copy in copies[len(small) + 3 :]:
        copy.wait()
    height = snaps * elements
    step = min(height, 256)
    for start in range(0, height, step):
        part = jnp.concatenate(
            [snapshots_ref.at[n].reshape(height, LANES)[start : start + step] for n in range(len(chunks))], axis=1
        )
        product_ref[start : start + step, :rows] = lax.dot_general(
            part, weighted, (((1,), (1,)), ((), ())), preferred_element_type=jnp.float32
        )
    turn = lax.broadcasted_iota(jnp.int32, (snaps, rows), 1) % elements
    chosen = jnp.zeros((snaps, rows), jnp.float32)
    for slot in range(elements):
        here = product_ref[pl.ds(slot, snaps, stride=elements), :][:, :rows]
        for elem in range(elements):
            chosen = jnp.where((turn == elem) & (map_ref[elem] == slot), here, chosen)
    for n in range(snaps // LANES):
        turned_ref[n * rows : (n + 1) * rows, :] = chosen[n * LANES : (n + 1) * LANES, :].T
    pair = 2 * own
    for n in range(snaps // LANES):
        total = turned_ref[pl.ds(n * rows, fields, stride=elements), :]
        for elem in range(1, elements):
            total += turned_ref[pl.ds(n * rows + elem, fields, stride=elements), :]
        for chip in range(n * LANES // pair, (n + 1) * LANES // pair):
            lane = chip * pair - n * LANES
            out_ref[pl.ds(chip, fields, stride=chips), :] = total[:, lane : lane + pair]


def partial_sums(velocity, geometry, mass, snapshots, eigvecs, mode_order, elem_map):
    fields, components, elements, points = velocity.shape
    snaps = snapshots.shape[0]
    own, mode_count = eigvecs.shape
    blocks = snaps // own
    r_rows, st = along_tables(points)
    chunks = components * (points // LANES)
    rows = fields * elements
    vmem = pl.BlockSpec(memory_space=pltpu.VMEM)
    return pl.pallas_call(
        functools.partial(partial_kernel, blocks),
        out_shape=(
            jax.ShapeDtypeStruct((fields * blocks // 2 + mode_count // 4, 2 * own), jnp.float32),
            jax.ShapeDtypeStruct((mode_count // 2, own), jnp.float32),
        ),
        in_specs=[pl.BlockSpec(memory_space=pltpu.HBM)] * 10,
        out_specs=(vmem, vmem),
        scratch_shapes=[
            pltpu.SMEM(elem_map.shape, jnp.int32),
            pltpu.VMEM((1, mode_count), jnp.int32),
            pltpu.VMEM((chunks, fields, elements, LANES), jnp.bfloat16),
            pltpu.VMEM(geometry.shape, jnp.float32),
            pltpu.VMEM(mass.shape, jnp.float32),
            pltpu.VMEM((1, points), jnp.float32),
            pltpu.VMEM(r_rows.shape, jnp.float32),
            pltpu.VMEM(st.shape, jnp.bfloat16),
            pltpu.VMEM(eigvecs.shape, jnp.float32),
            pltpu.VMEM((chunks, snaps, elements, LANES), jnp.bfloat16),
            pltpu.VMEM((snaps * elements, LANES), jnp.float32),
            pltpu.VMEM((snaps // LANES * rows, LANES), jnp.float32),
            pltpu.VMEM((mode_count, own), jnp.float32),
            pltpu.SemaphoreType.DMA((8 + 2 * chunks,)),
        ],
        compiler_params=pltpu.CompilerParams(vmem_limit_bytes=40 * 1024 * 1024),
    )(
        *[
            pltpu.with_memory_space_constraint(array, pltpu.HBM)
            for array in (
                elem_map,
                mode_order.reshape(1, mode_count),
                velocity,
                geometry,
                mass,
                jnp.asarray(point_weights()).reshape(1, points),
                jnp.asarray(r_rows),
                jnp.asarray(st),
                eigvecs,
                snapshots,
            )
        ]
    )


def exchange(block, ds, db):
    sections, blocks = lax.axis_size("sec"), lax.axis_size("blk")
    pairs = [
        (s * blocks + b, (s ^ ds) * blocks + (b ^ db))
        for s in range(sections)
        for b in range(blocks)
    ]
    return lax.ppermute(block, ("sec", "blk"), pairs)


def share_kernel(factor, chips, sums_ref, got_ref, held_ref, out_ref, total_ref):
    count = sums_ref.shape[0]
    fields, cols = out_ref.shape
    total_ref[...] = sums_ref[...] + got_ref[:count, :]
    chip = lax.axis_index("blk") // 2
    left = jnp.concatenate(
        [total_ref[pl.ds(chip ^ n, fields, stride=chips), :] for n in range(chips)], axis=1
    )
    right = [ref[start + n * cols : start + (n + 1) * cols, :] for ref, start in ((held_ref, 0), (got_ref, count)) for n in range(chips // 2)]
    out_ref[...] = factor * lax.dot_general(
        left,
        jnp.concatenate(right, axis=1),
        (((1,), (1,)), ((), ())),
        precision=lax.Precision.HIGHEST,
        preferred_element_type=jnp.float32,
    )


def shards(velocity, geometry, mass, snapshots, eigvecs, mode_order, elem_map):
    sections, blocks = lax.axis_size("sec"), lax.axis_size("blk")
    section, block = lax.axis_index("sec"), lax.axis_index("blk")
    fields, _, elements, _ = velocity.shape
    own, mode_count = eigvecs.shape
    chips, cols, pair = blocks // 2, mode_count // blocks, 2 * own
    factor = 0.25 / math.sqrt(elements * sections * blocks)

    packet, keep = partial_sums(velocity, geometry, mass, snapshots, eigvecs, mode_order, elem_map)
    got = exchange(packet, 0, 1)
    count = fields * chips
    sums = packet[:count] + got[:count]
    arrived = jnp.concatenate([got[count:, :own], got[count:, own:]], axis=0)
    second = (block & 1) != 0
    held = jnp.concatenate(
        [jnp.where(second, arrived, keep), jnp.where(second, keep, arrived)], axis=1
    ).reshape(chips, 1, cols, pair)

    step = sections // 2
    while step:
        count //= 2
        upper = (section & step) != 0
        low, high = sums[:count], sums[count:]
        sums = jnp.where(upper, high, low) + exchange(jnp.where(upper, low, high), step, 1)
        step //= 2

    step = 1
    while step < chips:
        halves = held.reshape((held.shape[0] // 2, 2) + held.shape[1:])
        upper = (block & (2 * step)) != 0
        held = jnp.where(upper, halves[:, 1], halves[:, 0])
        send = jnp.where(upper, halves[:, 0], halves[:, 1])
        got = exchange(jnp.concatenate([sums, send.reshape(-1, pair)], axis=0), 0, (2 * step) | 1)
        step *= 2
        if step < chips:
            held = jnp.concatenate([held, got[count:].reshape(held.shape)], axis=1)
            sums = sums + got[:count]

    held = held.reshape(-1, pair)
    if pair % LANES:
        total = (sums + got[:count]).reshape(count // chips, chips, pair)
        order = (block // 2) ^ jnp.arange(chips, dtype=jnp.int32)
        return factor * lax.dot_general(
            jnp.take(total, order, axis=1),
            jnp.concatenate([held, got[count:]], axis=0).reshape(chips, cols, pair),
            (((1, 2), (0, 2)), ((), ())),
            precision=lax.Precision.HIGHEST,
        )
    vmem = pl.BlockSpec(memory_space=pltpu.VMEM)
    return pl.pallas_call(
        functools.partial(share_kernel, factor, chips),
        out_shape=jax.ShapeDtypeStruct((count // chips, cols), jnp.float32),
        in_specs=[vmem] * 3,
        out_specs=vmem,
        scratch_shapes=[pltpu.VMEM((count, pair), jnp.float32)],
    )(*[pltpu.with_memory_space_constraint(array, pltpu.VMEM) for array in (sums, got, held)])


def solution(mesh):
    placed = (
        P(None, None, ("sec", "blk"), None),
        P(None, ("sec", "blk"), None),
        P(("sec", "blk"), None),
        P(None, None, ("sec", "blk"), None),
        P("blk", None),
        P(),
        P(("sec", "blk")),
    )
    return jax.shard_map(
        shards, mesh=mesh, in_specs=placed, out_specs=P("sec", "blk"), check_vma=False
    )
```

```python
import functools
import math

import jax
import jax.numpy as jnp
import numpy as np
from jax import lax
from jax.experimental import pallas as pl
from jax.experimental.pallas import tpu as pltpu
from jax.sharding import PartitionSpec as P

LANES = 128

GLL_NODES = np.array(
    [
        -1.0,
        -0.8717401485096066,
        -0.5917001814331423,
        -0.2092992179024789,
        0.2092992179024789,
        0.5917001814331423,
        0.8717401485096066,
        1.0,
    ]
)
GLL_WEIGHTS = np.array(
    [
        1.0 / 28.0,
        0.2107042271435061,
        0.3411226924835044,
        0.4124587946587038,
        0.4124587946587038,
        0.3411226924835044,
        0.2107042271435061,
        1.0 / 28.0,
    ]
)


def legendre_seven(nodes):
    before = nodes * 0.0 + 1.0
    current = nodes * 1.0
    for order in range(1, 7):
        following = ((2.0 * order + 1.0) * nodes * current - order * before) / (order + 1.0)
        before = current
        current = following
    return current


def derivative_matrix():
    degree = 7
    values = legendre_seven(GLL_NODES)
    result = np.zeros((8, 8))
    for row_idx in range(8):
        for col_idx in range(8):
            if row_idx != col_idx:
                result[row_idx, col_idx] = values[row_idx] / (
                    values[col_idx] * (GLL_NODES[row_idx] - GLL_NODES[col_idx])
                )
    result[0, 0] = -degree * (degree + 1) / 4.0
    result[7, 7] = degree * (degree + 1) / 4.0
    return result.astype(np.float32)


def point_weights():
    cube = GLL_WEIGHTS[:, None, None] * GLL_WEIGHTS[None, :, None] * GLL_WEIGHTS[None, None, :]
    return cube.reshape(512).astype(np.float32)


def along_tables(points):
    table = derivative_matrix()
    side = table.shape[0]
    lanes = np.arange(LANES)
    per_block = LANES // (side * side)
    i, j, k = lanes // (side * side), lanes // side % side, lanes % side
    along_s = table[j[None, :], j[:, None]] * (i[None, :] == i[:, None]) * (k[None, :] == k[:, None])
    along_t = table[k[None, :], k[:, None]] * (i[None, :] == i[:, None]) * (j[None, :] == j[:, None])
    along_r = [table[p * per_block + i, node] for p in range(points // LANES) for node in range(side)]
    return np.concatenate(
        [along_s, along_t, np.stack(along_r), point_weights().reshape(-1, LANES)], axis=0
    ).astype(np.float32)


def halves_of(values):
    high = values.astype(jnp.bfloat16)
    return high, (values - high.astype(jnp.float32)).astype(jnp.bfloat16)


def pair_rows(rows, height):
    elements = rows.shape[0]
    turn = lax.broadcasted_iota(jnp.int32, (height, LANES), 0) % elements
    spread = jnp.broadcast_to(rows[0:1], (height, LANES))
    for elem in range(1, elements):
        spread = jnp.where(turn == elem, rows[elem : elem + 1], spread)
    return spread


def parity(chip):
    return bin(chip).count("1") & 1


def odd_block(block, blocks):
    odd, rest = block & 1, blocks // 2
    while rest > 1:
        block = block >> 1
        odd = odd ^ (block & 1)
        rest //= 2
    return odd


def partial_kernel(
    blocks,
    map_hbm,
    order_hbm,
    velocity_hbm,
    geometry_hbm,
    mass_hbm,
    table_hbm,
    eigvecs_hbm,
    snapshots_hbm,
    out_ref,
    keep_ref,
    map_ref,
    order_ref,
    velocity_ref,
    geometry_ref,
    mass_ref,
    table_ref,
    eigvecs_ref,
    snapshots_ref,
    product_ref,
    columns_ref,
    semaphores,
):
    fields, components, elements, points = velocity_hbm.shape
    snaps = snapshots_hbm.shape[0]
    own, mode_count = eigvecs_hbm.shape
    parts = points // LANES
    rows = fields * elements
    chunks = [(c, p) for c in range(components) for p in range(parts)]
    small = [
        (velocity_hbm, velocity_ref),
        (table_hbm, table_ref),
        (geometry_hbm, geometry_ref),
        (mass_hbm, mass_ref),
        (order_hbm, order_ref),
        (eigvecs_hbm, eigvecs_ref),
        (map_hbm, map_ref),
    ]
    large = [
        (snapshots_hbm.at[:, c, :, pl.ds(p * LANES, LANES)], snapshots_ref.at[n])
        for n, (c, p) in enumerate(chunks)
    ]
    copies = [
        pltpu.make_async_copy(source, target, semaphores.at[n])
        for n, (source, target) in enumerate(small + large)
    ]
    for copy in copies:
        copy.start()
    for copy in copies[: len(small)]:
        copy.wait()

    packed = [
        velocity_ref[:, c, :, p * LANES : (p + 1) * LANES].reshape(rows, LANES) for c, p in chunks
    ]
    stacked = jnp.concatenate(packed, axis=0)
    st_high, st_low = halves_of(jnp.concatenate([table_ref[:LANES, :], table_ref[LANES : 2 * LANES, :]], axis=1))
    along_st = jnp.dot(
        jnp.concatenate([stacked, stacked], axis=1),
        jnp.concatenate([st_high, st_low], axis=0),
        preferred_element_type=jnp.float32,
    )
    point_row = table_hbm.shape[0] - parts
    side = (point_row - 2 * LANES) // parts
    lower = lax.broadcasted_iota(jnp.int32, (rows, LANES), 1) < LANES // 2
    along_r = []
    for c in range(components):
        nodes = []
        for p in range(parts):
            here = packed[c * parts + p].astype(jnp.float32)
            other = pltpu.roll(here, LANES // 2, 1)
            nodes += [jnp.where(lower, here, other), jnp.where(lower, other, here)]
        for p in range(parts):
            first = 2 * LANES + p * side
            total = table_ref[first : first + 1, :] * nodes[0]
            for node in range(1, side):
                total += table_ref[first + node : first + node + 1, :] * nodes[node]
            along_r.append(total)

    weighted = [None] * len(chunks)
    for p in range(parts):
        lanes = slice(p * LANES, (p + 1) * LANES)
        weight = mass_ref[:, lanes] * table_ref[point_row + p : point_row + p + 1, :]
        factors = [pair_rows(weight * geometry_ref[n, :, lanes], rows) for n in range(9)]

        def gradient(component, coord):
            row = (component * parts + p) * rows
            part = along_st[row : row + rows]
            return (
                factors[coord] * along_r[component * parts + p]
                + factors[3 + coord] * part[:, :LANES]
                + factors[6 + coord] * part[:, LANES:]
            )

        for c in range(components):
            after, last = (c + 1) % 3, (c + 2) % 3
            weighted[c * parts + p] = (gradient(last, after) - gradient(after, last)).astype(jnp.bfloat16)

    selector = (
        lax.broadcasted_iota(jnp.int32, (mode_count, mode_count), 0) == order_ref[...]
    ).astype(jnp.bfloat16)
    columns_ref[...] = sum(
        jnp.dot(piece, selector, preferred_element_type=jnp.float32) for piece in halves_of(eigvecs_ref[...])
    ).T
    cols, chips = mode_count // blocks, blocks // 2
    odd = odd_block(lax.axis_index("blk"), blocks)
    half = mode_count // 4
    first = fields * chips
    for chip in range(chips):
        even = parity(chip)
        keep = columns_ref[pl.ds((2 * chip + (even ^ odd)) * cols, cols), :]
        send = columns_ref[pl.ds((2 * chip + (even ^ 1 ^ odd)) * cols, cols), :]
        keep_ref[chip * cols : (chip + 1) * cols, :] = keep
        row, lane = chip * cols % half, chip * cols // half * own
        out_ref[first + row : first + row + cols, lane : lane + own] = send

    width = LANES * elements
    spans = snaps // LANES
    adder = (
        lax.broadcasted_iota(jnp.int32, (width, LANES), 0) // elements
        == lax.broadcasted_iota(jnp.int32, (width, LANES), 1)
    ).astype(jnp.bfloat16)
    slot = lax.broadcasted_iota(jnp.int32, (fields, LANES), 1) % elements
    for c in range(components):
        group = range(c * parts, (c + 1) * parts)
        for n in group:
            copies[len(small) + n].wait()
        values = jnp.concatenate([weighted[n] for n in group], axis=1)
        for span in range(spans):
            part = jnp.concatenate(
                [
                    snapshots_ref.at[n].reshape(snaps * elements, LANES)[span * width : (span + 1) * width]
                    for n in group
                ],
                axis=1,
            )
            product = lax.dot_general(values, part, (((1,), (1,)), ((), ())), preferred_element_type=jnp.float32)
            for piece in range(elements):
                place = slice((span * elements + piece) * rows, (span * elements + piece + 1) * rows)
                added = product[:, piece * LANES : (piece + 1) * LANES]
                product_ref[place, :] = added + product_ref[place, :] if c else added
    matched = []
    for block in range(spans * elements):
        chosen = product_ref[pl.ds(block * rows, fields, stride=elements), :]
        for elem in range(1, elements):
            here = product_ref[pl.ds(block * rows + elem, fields, stride=elements), :]
            chosen = jnp.where(slot == map_ref[elem], here, chosen)
        matched.append(halves_of(chosen))
    matched = [
        jnp.concatenate([matched[span * elements + piece][part] for piece in range(elements)], axis=1)
        for span in range(spans)
        for part in range(2)
    ]
    totals = jnp.dot(jnp.concatenate(matched, axis=0), adder, preferred_element_type=jnp.float32)
    pair = 2 * own
    for span in range(spans):
        row = 2 * span * fields
        total = totals[row : row + fields] + totals[row + fields : row + 2 * fields]
        for lane in range(0, LANES, pair):
            chip = (span * LANES + lane) // pair
            out_ref[pl.ds(chip, fields, stride=chips), :] = total[:, lane : lane + pair]


def partial_sums(velocity, geometry, mass, snapshots, eigvecs, mode_order, elem_map):
    fields, components, elements, points = velocity.shape
    snaps = snapshots.shape[0]
    own, mode_count = eigvecs.shape
    blocks = snaps // own
    table = along_tables(points)
    chunks = components * (points // LANES)
    vmem = pl.BlockSpec(memory_space=pltpu.VMEM)
    return pl.pallas_call(
        functools.partial(partial_kernel, blocks),
        out_shape=(
            jax.ShapeDtypeStruct((fields * blocks // 2 + mode_count // 4, 2 * own), jnp.float32),
            jax.ShapeDtypeStruct((mode_count // 2, own), jnp.float32),
        ),
        in_specs=[pl.BlockSpec(memory_space=pltpu.HBM)] * 8,
        out_specs=(vmem, vmem),
        scratch_shapes=[
            pltpu.SMEM(elem_map.shape, jnp.int32),
            pltpu.VMEM((1, mode_count), jnp.int32),
            pltpu.VMEM(velocity.shape, jnp.bfloat16),
            pltpu.VMEM(geometry.shape, jnp.float32),
            pltpu.VMEM(mass.shape, jnp.float32),
            pltpu.VMEM(table.shape, jnp.float32),
            pltpu.VMEM(eigvecs.shape, jnp.float32),
            pltpu.VMEM((chunks, snaps, elements, LANES), jnp.bfloat16),
            pltpu.VMEM((snaps * elements // LANES * fields * elements, LANES), jnp.float32),
            pltpu.VMEM((mode_count, own), jnp.float32),
            pltpu.SemaphoreType.DMA((7 + chunks,)),
        ],
        compiler_params=pltpu.CompilerParams(vmem_limit_bytes=40 * 1024 * 1024),
    )(
        *[
            pltpu.with_memory_space_constraint(array, pltpu.HBM)
            for array in (
                elem_map,
                mode_order.reshape(1, mode_count),
                velocity,
                geometry,
                mass,
                jnp.asarray(table),
                eigvecs,
                snapshots,
            )
        ]
    )


def exchange(block, ds, db):
    sections, blocks = lax.axis_size("sec"), lax.axis_size("blk")
    pairs = [
        (s * blocks + b, (s ^ ds) * blocks + (b ^ db))
        for s in range(sections)
        for b in range(blocks)
    ]
    return lax.ppermute(block, ("sec", "blk"), pairs)


def share_kernel(factor, chips, sums_ref, got_ref, held_ref, out_ref, total_ref):
    count = sums_ref.shape[0]
    fields, cols = out_ref.shape
    total_ref[...] = sums_ref[...] + got_ref[:count, :]
    chip = lax.axis_index("blk") // 2
    left = jnp.concatenate(
        [total_ref[pl.ds(chip ^ n, fields, stride=chips), :] for n in range(chips)], axis=1
    )
    right = [ref[start + n * cols : start + (n + 1) * cols, :] for ref, start in ((held_ref, 0), (got_ref, count)) for n in range(chips // 2)]
    out_ref[...] = factor * lax.dot_general(
        left,
        jnp.concatenate(right, axis=1),
        (((1,), (1,)), ((), ())),
        precision=lax.Precision.HIGHEST,
        preferred_element_type=jnp.float32,
    )


def shards(velocity, geometry, mass, snapshots, eigvecs, mode_order, elem_map):
    sections, blocks = lax.axis_size("sec"), lax.axis_size("blk")
    section, block = lax.axis_index("sec"), lax.axis_index("blk")
    fields, _, elements, _ = velocity.shape
    own, mode_count = eigvecs.shape
    chips, cols, pair = blocks // 2, mode_count // blocks, 2 * own
    factor = 0.25 / math.sqrt(elements * sections * blocks)

    packet, keep = partial_sums(velocity, geometry, mass, snapshots, eigvecs, mode_order, elem_map)
    got = exchange(packet, 0, 1)
    count = fields * chips
    sums = packet[:count] + got[:count]
    arrived = jnp.concatenate([got[count:, :own], got[count:, own:]], axis=0)
    second = (block & 1) != 0
    held = jnp.concatenate(
        [jnp.where(second, arrived, keep), jnp.where(second, keep, arrived)], axis=1
    ).reshape(chips, 1, cols, pair)

    step = sections // 2
    while step:
        count //= 2
        upper = (section & step) != 0
        low, high = sums[:count], sums[count:]
        sums = jnp.where(upper, high, low) + exchange(jnp.where(upper, low, high), step, 1)
        step //= 2

    step = 1
    while step < chips:
        halves = held.reshape((held.shape[0] // 2, 2) + held.shape[1:])
        upper = (block & (2 * step)) != 0
        held = jnp.where(upper, halves[:, 1], halves[:, 0])
        send = jnp.where(upper, halves[:, 0], halves[:, 1])
        got = exchange(jnp.concatenate([sums, send.reshape(-1, pair)], axis=0), 0, (2 * step) | 1)
        step *= 2
        if step < chips:
            held = jnp.concatenate([held, got[count:].reshape(held.shape)], axis=1)
            sums = sums + got[:count]

    held = held.reshape(-1, pair)
    if pair % LANES:
        total = (sums + got[:count]).reshape(count // chips, chips, pair)
        order = (block // 2) ^ jnp.arange(chips, dtype=jnp.int32)
        return factor * lax.dot_general(
            jnp.take(total, order, axis=1),
            jnp.concatenate([held, got[count:]], axis=0).reshape(chips, cols, pair),
            (((1, 2), (0, 2)), ((), ())),
            precision=lax.Precision.HIGHEST,
        )
    vmem = pl.BlockSpec(memory_space=pltpu.VMEM)
    return pl.pallas_call(
        functools.partial(share_kernel, factor, chips),
        out_shape=jax.ShapeDtypeStruct((count // chips, cols), jnp.float32),
        in_specs=[vmem] * 3,
        out_specs=vmem,
        scratch_shapes=[pltpu.VMEM((count, pair), jnp.float32)],
    )(*[pltpu.with_memory_space_constraint(array, pltpu.VMEM) for array in (sums, got, held)])


def solution(mesh):
    placed = (
        P(None, None, ("sec", "blk"), None),
        P(None, ("sec", "blk"), None),
        P(("sec", "blk"), None),
        P(None, None, ("sec", "blk"), None),
        P("blk", None),
        P(),
        P(("sec", "blk")),
    )
    return jax.shard_map(
        shards, mesh=mesh, in_specs=placed, out_specs=P("sec", "blk"), check_vma=False
    )
```

```python
import functools
import math

import jax
import jax.numpy as jnp
import numpy as np
from jax import lax
from jax.experimental import pallas as pl
from jax.experimental.pallas import tpu as pltpu
from jax.sharding import PartitionSpec as P

LANES = 128

GLL_NODES = np.array(
    [
        -1.0,
        -0.8717401485096066,
        -0.5917001814331423,
        -0.2092992179024789,
        0.2092992179024789,
        0.5917001814331423,
        0.8717401485096066,
        1.0,
    ]
)
GLL_WEIGHTS = np.array(
    [
        1.0 / 28.0,
        0.2107042271435061,
        0.3411226924835044,
        0.4124587946587038,
        0.4124587946587038,
        0.3411226924835044,
        0.2107042271435061,
        1.0 / 28.0,
    ]
)


def legendre_seven(nodes):
    before = nodes * 0.0 + 1.0
    current = nodes * 1.0
    for order in range(1, 7):
        following = ((2.0 * order + 1.0) * nodes * current - order * before) / (order + 1.0)
        before = current
        current = following
    return current


def derivative_matrix():
    degree = 7
    values = legendre_seven(GLL_NODES)
    result = np.zeros((8, 8))
    for row_idx in range(8):
        for col_idx in range(8):
            if row_idx != col_idx:
                result[row_idx, col_idx] = values[row_idx] / (
                    values[col_idx] * (GLL_NODES[row_idx] - GLL_NODES[col_idx])
                )
    result[0, 0] = -degree * (degree + 1) / 4.0
    result[7, 7] = degree * (degree + 1) / 4.0
    return result.astype(np.float32)


def point_weights():
    cube = GLL_WEIGHTS[:, None, None] * GLL_WEIGHTS[None, :, None] * GLL_WEIGHTS[None, None, :]
    return cube.reshape(512).astype(np.float32)


def along_tables(points):
    table = derivative_matrix()
    side = table.shape[0]
    lanes = np.arange(LANES)
    per_block = LANES // (side * side)
    i, j, k = lanes // (side * side), lanes // side % side, lanes % side
    along_s = table[j[None, :], j[:, None]] * (i[None, :] == i[:, None]) * (k[None, :] == k[:, None])
    along_t = table[k[None, :], k[:, None]] * (i[None, :] == i[:, None]) * (j[None, :] == j[:, None])
    along_r = [table[p * per_block + i, node] for p in range(points // LANES) for node in range(side)]
    return np.concatenate(
        [along_s, along_t, np.stack(along_r), point_weights().reshape(-1, LANES)], axis=0
    ).astype(np.float32)


def halves_of(values):
    high = values.astype(jnp.bfloat16)
    return high, (values - high.astype(jnp.float32)).astype(jnp.bfloat16)


def pair_rows(rows, height):
    elements = rows.shape[0]
    turn = lax.broadcasted_iota(jnp.int32, (height, LANES), 0) % elements
    spread = jnp.broadcast_to(rows[0:1], (height, LANES))
    for elem in range(1, elements):
        spread = jnp.where(turn == elem, rows[elem : elem + 1], spread)
    return spread


def parity(chip):
    return bin(chip).count("1") & 1


def odd_block(block, blocks):
    odd, rest = block & 1, blocks // 2
    while rest > 1:
        block = block >> 1
        odd = odd ^ (block & 1)
        rest //= 2
    return odd


def stored_kernel(
    blocks,
    map_hbm,
    order_hbm,
    velocity_hbm,
    geometry_hbm,
    mass_hbm,
    table_hbm,
    eigvecs_hbm,
    stored_ref,
    send_ref,
    keep_ref,
    map_ref,
    order_ref,
    velocity_ref,
    geometry_ref,
    mass_ref,
    table_ref,
    eigvecs_ref,
    columns_ref,
    semaphores,
):
    fields, components, elements, points = velocity_hbm.shape
    own, mode_count = eigvecs_hbm.shape
    parts = points // LANES
    rows = fields * elements
    chunks = [(c, p) for c in range(components) for p in range(parts)]
    small = [
        (velocity_hbm, velocity_ref),
        (table_hbm, table_ref),
        (geometry_hbm, geometry_ref),
        (mass_hbm, mass_ref),
        (order_hbm, order_ref),
        (eigvecs_hbm, eigvecs_ref),
        (map_hbm, map_ref),
    ]
    copies = [
        pltpu.make_async_copy(source, target, semaphores.at[n])
        for n, (source, target) in enumerate(small)
    ]
    for copy in copies:
        copy.start()
    for copy in copies:
        copy.wait()

    packed = [
        velocity_ref[:, c, :, p * LANES : (p + 1) * LANES].reshape(rows, LANES) for c, p in chunks
    ]
    stacked = jnp.concatenate(packed, axis=0)
    st_high, st_low = halves_of(jnp.concatenate([table_ref[:LANES, :], table_ref[LANES : 2 * LANES, :]], axis=1))
    along_st = jnp.dot(
        jnp.concatenate([stacked, stacked], axis=1),
        jnp.concatenate([st_high, st_low], axis=0),
        preferred_element_type=jnp.float32,
    )
    point_row = table_hbm.shape[0] - parts
    side = (point_row - 2 * LANES) // parts
    lower = lax.broadcasted_iota(jnp.int32, (rows, LANES), 1) < LANES // 2
    along_r = []
    for c in range(components):
        nodes = []
        for p in range(parts):
            here = packed[c * parts + p].astype(jnp.float32)
            other = pltpu.roll(here, LANES // 2, 1)
            nodes += [jnp.where(lower, here, other), jnp.where(lower, other, here)]
        for p in range(parts):
            first = 2 * LANES + p * side
            total = table_ref[first : first + 1, :] * nodes[0]
            for node in range(1, side):
                total += table_ref[first + node : first + node + 1, :] * nodes[node]
            along_r.append(total)

    straight = map_ref[0] == 0
    first_row = lax.broadcasted_iota(jnp.int32, (rows, LANES), 0) % elements == 0
    for p in range(parts):
        lanes = slice(p * LANES, (p + 1) * LANES)
        weight = mass_ref[:, lanes] * table_ref[point_row + p : point_row + p + 1, :]
        factors = [pair_rows(weight * geometry_ref[n, :, lanes], rows) for n in range(9)]

        def gradient(component, coord):
            row = (component * parts + p) * rows
            part = along_st[row : row + rows]
            return (
                factors[coord] * along_r[component * parts + p]
                + factors[3 + coord] * part[:, :LANES]
                + factors[6 + coord] * part[:, LANES:]
            )

        for c in range(components):
            after, last = (c + 1) % 3, (c + 2) % 3
            values = gradient(last, after) - gradient(after, last)
            turned = jnp.where(first_row, pltpu.roll(values, rows - 1, 0), pltpu.roll(values, 1, 0))
            values = jnp.where(straight, values, turned).astype(jnp.bfloat16)
            stored_ref[:, c, :, lanes] = values.reshape(fields, elements, LANES)

    selector = (
        lax.broadcasted_iota(jnp.int32, (mode_count, mode_count), 0) == order_ref[...]
    ).astype(jnp.bfloat16)
    columns_ref[...] = sum(
        jnp.dot(piece, selector, preferred_element_type=jnp.float32) for piece in halves_of(eigvecs_ref[...])
    ).T
    cols, chips = mode_count // blocks, blocks // 2
    odd = odd_block(lax.axis_index("blk"), blocks)
    half = mode_count // 4
    for chip in range(chips):
        even = parity(chip)
        keep = columns_ref[pl.ds((2 * chip + (even ^ odd)) * cols, cols), :]
        send = columns_ref[pl.ds((2 * chip + (even ^ 1 ^ odd)) * cols, cols), :]
        keep_ref[chip * cols : (chip + 1) * cols, :] = keep
        row, lane = chip * cols % half, chip * cols // half * own
        send_ref[row : row + cols, lane : lane + own] = send


def stored_vorticity(velocity, geometry, mass, eigvecs, mode_order, elem_map):
    fields, components, elements, points = velocity.shape
    own, mode_count = eigvecs.shape
    blocks = lax.axis_size("blk")
    table = along_tables(points)
    vmem = pl.BlockSpec(memory_space=pltpu.VMEM)
    return pl.pallas_call(
        functools.partial(stored_kernel, blocks),
        out_shape=(
            pltpu.VMEM(velocity.shape, jnp.bfloat16),
            pltpu.VMEM((mode_count // 4, 2 * own), jnp.float32),
            pltpu.VMEM((mode_count // 2, own), jnp.float32),
        ),
        in_specs=[pl.BlockSpec(memory_space=pltpu.HBM)] * 7,
        out_specs=(vmem,) * 3,
        scratch_shapes=[
            pltpu.SMEM(elem_map.shape, jnp.int32),
            pltpu.VMEM((1, mode_count), jnp.int32),
            pltpu.VMEM(velocity.shape, jnp.bfloat16),
            pltpu.VMEM(geometry.shape, jnp.float32),
            pltpu.VMEM(mass.shape, jnp.float32),
            pltpu.VMEM(table.shape, jnp.float32),
            pltpu.VMEM(eigvecs.shape, jnp.float32),
            pltpu.VMEM((mode_count, own), jnp.float32),
            pltpu.SemaphoreType.DMA((7,)),
        ],
    )(
        *[
            pltpu.with_memory_space_constraint(array, pltpu.HBM)
            for array in (
                elem_map,
                mode_order.reshape(1, mode_count),
                velocity,
                geometry,
                mass,
                jnp.asarray(table),
                eigvecs,
            )
        ]
    )


def exchange(block, ds, db):
    sections, blocks = lax.axis_size("sec"), lax.axis_size("blk")
    pairs = [
        (s * blocks + b, (s ^ ds) * blocks + (b ^ db))
        for s in range(sections)
        for b in range(blocks)
    ]
    return lax.ppermute(block, ("sec", "blk"), pairs)


def share_kernel(factor, chips, sums_ref, got_ref, held_ref, out_ref, total_ref):
    count = sums_ref.shape[0]
    fields, cols = out_ref.shape
    total_ref[...] = sums_ref[...] + got_ref[:count, :]
    chip = lax.axis_index("blk") // 2
    left = jnp.concatenate(
        [total_ref[pl.ds(chip ^ n, fields, stride=chips), :] for n in range(chips)], axis=1
    )
    right = [ref[start + n * cols : start + (n + 1) * cols, :] for ref, start in ((held_ref, 0), (got_ref, count)) for n in range(chips // 2)]
    out_ref[...] = factor * lax.dot_general(
        left,
        jnp.concatenate(right, axis=1),
        (((1,), (1,)), ((), ())),
        precision=lax.Precision.HIGHEST,
        preferred_element_type=jnp.float32,
    )


def shards(velocity, geometry, mass, snapshots, eigvecs, mode_order, elem_map):
    sections, blocks = lax.axis_size("sec"), lax.axis_size("blk")
    section, block = lax.axis_index("sec"), lax.axis_index("blk")
    fields, _, elements, _ = velocity.shape
    own, mode_count = eigvecs.shape
    chips, cols, pair = blocks // 2, mode_count // blocks, 2 * own
    factor = 0.25 / math.sqrt(elements * sections * blocks)

    stored, send, keep = stored_vorticity(velocity, geometry, mass, eigvecs, mode_order, elem_map)
    sums = lax.dot_general(
        stored.reshape(fields, -1),
        snapshots.reshape(snapshots.shape[0], -1),
        (((1,), (1,)), ((), ())),
        preferred_element_type=jnp.float32,
    ).reshape(-1, pair)
    count = fields * chips
    got = exchange(jnp.concatenate([sums, send], axis=0), 0, 1)
    sums = sums + got[:count]
    arrived = jnp.concatenate([got[count:, :own], got[count:, own:]], axis=0)
    second = (block & 1) != 0
    held = jnp.concatenate(
        [jnp.where(second, arrived, keep), jnp.where(second, keep, arrived)], axis=1
    ).reshape(chips, 1, cols, pair)

    step = sections // 2
    while step:
        count //= 2
        upper = (section & step) != 0
        low, high = sums[:count], sums[count:]
        sums = jnp.where(upper, high, low) + exchange(jnp.where(upper, low, high), step, 1)
        step //= 2

    step = 1
    while step < chips:
        halves = held.reshape((held.shape[0] // 2, 2) + held.shape[1:])
        upper = (block & (2 * step)) != 0
        held = jnp.where(upper, halves[:, 1], halves[:, 0])
        send = jnp.where(upper, halves[:, 0], halves[:, 1])
        got = exchange(jnp.concatenate([sums, send.reshape(-1, pair)], axis=0), 0, (2 * step) | 1)
        step *= 2
        if step < chips:
            held = jnp.concatenate([held, got[count:].reshape(held.shape)], axis=1)
            sums = sums + got[:count]

    held = held.reshape(-1, pair)
    if pair % LANES:
        total = (sums + got[:count]).reshape(count // chips, chips, pair)
        order = (block // 2) ^ jnp.arange(chips, dtype=jnp.int32)
        return factor * lax.dot_general(
            jnp.take(total, order, axis=1),
            jnp.concatenate([held, got[count:]], axis=0).reshape(chips, cols, pair),
            (((1, 2), (0, 2)), ((), ())),
            precision=lax.Precision.HIGHEST,
        )
    vmem = pl.BlockSpec(memory_space=pltpu.VMEM)
    return pl.pallas_call(
        functools.partial(share_kernel, factor, chips),
        out_shape=jax.ShapeDtypeStruct((count // chips, cols), jnp.float32),
        in_specs=[vmem] * 3,
        out_specs=vmem,
        scratch_shapes=[pltpu.VMEM((count, pair), jnp.float32)],
    )(*[pltpu.with_memory_space_constraint(array, pltpu.VMEM) for array in (sums, got, held)])


def solution(mesh):
    placed = (
        P(None, None, ("sec", "blk"), None),
        P(None, ("sec", "blk"), None),
        P(("sec", "blk"), None),
        P(None, None, ("sec", "blk"), None),
        P("blk", None),
        P(),
        P(("sec", "blk")),
    )
    return jax.shard_map(
        shards, mesh=mesh, in_specs=placed, out_specs=P("sec", "blk"), check_vma=False
    )
```

```python
import functools
import math

import jax
import jax.numpy as jnp
import numpy as np
from jax import lax
from jax.experimental import pallas as pl
from jax.experimental.pallas import tpu as pltpu
from jax.sharding import PartitionSpec as P

LANES = 128

GLL_NODES = np.array(
    [
        -1.0,
        -0.8717401485096066,
        -0.5917001814331423,
        -0.2092992179024789,
        0.2092992179024789,
        0.5917001814331423,
        0.8717401485096066,
        1.0,
    ]
)
GLL_WEIGHTS = np.array(
    [
        1.0 / 28.0,
        0.2107042271435061,
        0.3411226924835044,
        0.4124587946587038,
        0.4124587946587038,
        0.3411226924835044,
        0.2107042271435061,
        1.0 / 28.0,
    ]
)


def legendre_seven(nodes):
    before = nodes * 0.0 + 1.0
    current = nodes * 1.0
    for order in range(1, 7):
        following = ((2.0 * order + 1.0) * nodes * current - order * before) / (order + 1.0)
        before = current
        current = following
    return current


def derivative_matrix():
    degree = 7
    values = legendre_seven(GLL_NODES)
    result = np.zeros((8, 8))
    for row_idx in range(8):
        for col_idx in range(8):
            if row_idx != col_idx:
                result[row_idx, col_idx] = values[row_idx] / (
                    values[col_idx] * (GLL_NODES[row_idx] - GLL_NODES[col_idx])
                )
    result[0, 0] = -degree * (degree + 1) / 4.0
    result[7, 7] = degree * (degree + 1) / 4.0
    return result.astype(np.float32)


def point_weights():
    cube = GLL_WEIGHTS[:, None, None] * GLL_WEIGHTS[None, :, None] * GLL_WEIGHTS[None, None, :]
    return cube.reshape(512).astype(np.float32)


def along_tables(points):
    table = derivative_matrix()
    side = table.shape[0]
    lanes = np.arange(LANES)
    per_block = LANES // (side * side)
    i, j, k = lanes // (side * side), lanes // side % side, lanes % side
    along_s = table[j[None, :], j[:, None]] * (i[None, :] == i[:, None]) * (k[None, :] == k[:, None])
    along_t = table[k[None, :], k[:, None]] * (i[None, :] == i[:, None]) * (j[None, :] == j[:, None])
    along_r = [table[p * per_block + i, node] for p in range(points // LANES) for node in range(side)]
    return np.concatenate(
        [along_s, along_t, np.stack(along_r), point_weights().reshape(-1, LANES)], axis=0
    ).astype(np.float32)


def halves_of(values):
    high = values.astype(jnp.bfloat16)
    return high, (values - high.astype(jnp.float32)).astype(jnp.bfloat16)


def pair_rows(rows, height):
    elements = rows.shape[0]
    turn = lax.broadcasted_iota(jnp.int32, (height, LANES), 0) % elements
    spread = jnp.broadcast_to(rows[0:1], (height, LANES))
    for elem in range(1, elements):
        spread = jnp.where(turn == elem, rows[elem : elem + 1], spread)
    return spread


def stored_kernel(
    blocks,
    map_hbm,
    order_hbm,
    velocity_hbm,
    geometry_hbm,
    mass_hbm,
    table_hbm,
    eigvecs_hbm,
    stored_ref,
    send_ref,
    keep_ref,
    map_ref,
    order_ref,
    velocity_ref,
    geometry_ref,
    mass_ref,
    table_ref,
    eigvecs_ref,
    columns_ref,
    semaphores,
):
    fields, components, elements, points = velocity_hbm.shape
    own, mode_count = eigvecs_hbm.shape
    parts = points // LANES
    rows = fields * elements
    chunks = [(c, p) for c in range(components) for p in range(parts)]
    small = [
        (velocity_hbm, velocity_ref),
        (table_hbm, table_ref),
        (geometry_hbm, geometry_ref),
        (mass_hbm, mass_ref),
        (order_hbm, order_ref),
        (eigvecs_hbm, eigvecs_ref),
        (map_hbm, map_ref),
    ]
    copies = [
        pltpu.make_async_copy(source, target, semaphores.at[n])
        for n, (source, target) in enumerate(small)
    ]
    for copy in copies:
        copy.start()
    for copy in copies:
        copy.wait()

    packed = [
        velocity_ref[:, c, :, p * LANES : (p + 1) * LANES].reshape(rows, LANES) for c, p in chunks
    ]
    stacked = jnp.concatenate(packed, axis=0)
    st_high, st_low = halves_of(jnp.concatenate([table_ref[:LANES, :], table_ref[LANES : 2 * LANES, :]], axis=1))
    along_st = jnp.dot(
        jnp.concatenate([stacked, stacked], axis=1),
        jnp.concatenate([st_high, st_low], axis=0),
        preferred_element_type=jnp.float32,
    )
    point_row = table_hbm.shape[0] - parts
    side = (point_row - 2 * LANES) // parts
    lower = lax.broadcasted_iota(jnp.int32, (rows, LANES), 1) < LANES // 2
    along_r = []
    for c in range(components):
        nodes = []
        for p in range(parts):
            here = packed[c * parts + p].astype(jnp.float32)
            other = pltpu.roll(here, LANES // 2, 1)
            nodes += [jnp.where(lower, here, other), jnp.where(lower, other, here)]
        for p in range(parts):
            first = 2 * LANES + p * side
            total = table_ref[first : first + 1, :] * nodes[0]
            for node in range(1, side):
                total += table_ref[first + node : first + node + 1, :] * nodes[node]
            along_r.append(total)

    straight = map_ref[0] == 0
    first_row = lax.broadcasted_iota(jnp.int32, (rows, LANES), 0) % elements == 0
    for p in range(parts):
        lanes = slice(p * LANES, (p + 1) * LANES)
        weight = mass_ref[:, lanes] * table_ref[point_row + p : point_row + p + 1, :]
        factors = [pair_rows(weight * geometry_ref[n, :, lanes], rows) for n in range(9)]

        def gradient(component, coord):
            row = (component * parts + p) * rows
            part = along_st[row : row + rows]
            return (
                factors[coord] * along_r[component * parts + p]
                + factors[3 + coord] * part[:, :LANES]
                + factors[6 + coord] * part[:, LANES:]
            )

        for c in range(components):
            after, last = (c + 1) % 3, (c + 2) % 3
            values = gradient(last, after) - gradient(after, last)
            turned = jnp.where(first_row, pltpu.roll(values, rows - 1, 0), pltpu.roll(values, 1, 0))
            values = jnp.where(straight, values, turned).astype(jnp.bfloat16)
            stored_ref[:, c, :, lanes] = values.reshape(fields, elements, LANES)

    selector = (
        lax.broadcasted_iota(jnp.int32, (mode_count, mode_count), 0) == order_ref[...]
    ).astype(jnp.bfloat16)
    columns_ref[...] = sum(
        jnp.dot(piece, selector, preferred_element_type=jnp.float32) for piece in halves_of(eigvecs_ref[...])
    ).T
    cols, chips = mode_count // blocks, blocks // 2
    block = lax.axis_index("blk")
    core = block & 1
    half = mode_count // 4
    for chip in range(chips):
        kept = jnp.where(chip == block // 2, core, 1 - core)
        keep = columns_ref[pl.ds((2 * chip + kept) * cols, cols), :]
        send = columns_ref[pl.ds((2 * chip + 1 - kept) * cols, cols), :]
        keep_ref[chip * cols : (chip + 1) * cols, :] = keep
        row, lane = chip * cols % half, chip * cols // half * own
        send_ref[row : row + cols, lane : lane + own] = send


def stored_vorticity(velocity, geometry, mass, eigvecs, mode_order, elem_map):
    fields, components, elements, points = velocity.shape
    own, mode_count = eigvecs.shape
    blocks = lax.axis_size("blk")
    table = along_tables(points)
    vmem = pl.BlockSpec(memory_space=pltpu.VMEM)
    return pl.pallas_call(
        functools.partial(stored_kernel, blocks),
        out_shape=(
            pltpu.VMEM(velocity.shape, jnp.bfloat16),
            pltpu.VMEM((mode_count // 4, 2 * own), jnp.float32),
            pltpu.VMEM((mode_count // 2, own), jnp.float32),
        ),
        in_specs=[pl.BlockSpec(memory_space=pltpu.HBM)] * 7,
        out_specs=(vmem,) * 3,
        scratch_shapes=[
            pltpu.SMEM(elem_map.shape, jnp.int32),
            pltpu.VMEM((1, mode_count), jnp.int32),
            pltpu.VMEM(velocity.shape, jnp.bfloat16),
            pltpu.VMEM(geometry.shape, jnp.float32),
            pltpu.VMEM(mass.shape, jnp.float32),
            pltpu.VMEM(table.shape, jnp.float32),
            pltpu.VMEM(eigvecs.shape, jnp.float32),
            pltpu.VMEM((mode_count, own), jnp.float32),
            pltpu.SemaphoreType.DMA((7,)),
        ],
    )(
        *[
            pltpu.with_memory_space_constraint(array, pltpu.HBM)
            for array in (
                elem_map,
                mode_order.reshape(1, mode_count),
                velocity,
                geometry,
                mass,
                jnp.asarray(table),
                eigvecs,
            )
        ]
    )


def exchange(block, ds, db):
    sections, blocks = lax.axis_size("sec"), lax.axis_size("blk")
    pairs = [
        (s * blocks + b, (s ^ ds) * blocks + (b ^ db))
        for s in range(sections)
        for b in range(blocks)
    ]
    return lax.ppermute(block, ("sec", "blk"), pairs)


def share_kernel(factor, others, sums_ref, held_ref, *refs):
    *got_refs, out_ref, total_ref = refs
    count, chips = sums_ref.shape[0], len(others) + 1
    fields = out_ref.shape[0]
    total = sums_ref[...]
    for got_ref in got_refs:
        total += got_ref[:count, :]
    total_ref[...] = total
    chip = lax.axis_index("blk") // 2
    left = [total_ref[pl.ds(chip ^ other, fields, stride=chips), :] for other in (0, *others)]
    right = [held_ref[...]] + [got_ref[count:, :] for got_ref in got_refs]
    out_ref[...] = factor * lax.dot_general(
        jnp.concatenate(left, axis=1),
        jnp.concatenate(right, axis=1),
        (((1,), (1,)), ((), ())),
        precision=lax.Precision.HIGHEST,
        preferred_element_type=jnp.float32,
    )


def shards(velocity, geometry, mass, snapshots, eigvecs, mode_order, elem_map):
    sections, blocks = lax.axis_size("sec"), lax.axis_size("blk")
    section, block = lax.axis_index("sec"), lax.axis_index("blk")
    fields, _, elements, _ = velocity.shape
    own, mode_count = eigvecs.shape
    chips, cols, pair = blocks // 2, mode_count // blocks, 2 * own
    factor = 0.25 / math.sqrt(elements * sections * blocks)

    stored, send, keep = stored_vorticity(velocity, geometry, mass, eigvecs, mode_order, elem_map)
    sums = lax.dot_general(
        stored.reshape(fields, -1),
        snapshots.reshape(snapshots.shape[0], -1),
        (((1,), (1,)), ((), ())),
        preferred_element_type=jnp.float32,
    ).reshape(-1, pair)
    count = fields * chips
    got = exchange(jnp.concatenate([sums, send], axis=0), 0, 1)
    sums = sums + got[:count]
    arrived = jnp.concatenate([got[count:, :own], got[count:, own:]], axis=0)
    second = (block & 1) != 0
    held = jnp.concatenate(
        [jnp.where(second, arrived, keep), jnp.where(second, keep, arrived)], axis=1
    ).reshape(chips, cols, pair)

    step = sections // 2
    while step:
        count //= 2
        upper = (section & step) != 0
        low, high = sums[:count], sums[count:]
        sums = jnp.where(upper, high, low) + exchange(jnp.where(upper, low, high), step, 1)
        step //= 2

    others = [n for n in (2,3,1) if n < chips] + list(range(4, chips))
    chip = block // 2
    got = []
    for other in others:
        packet = jnp.concatenate([sums, lax.dynamic_index_in_dim(held, chip ^ other, 0, keepdims=False)], axis=0)
        got.append(exchange(packet, 0, 2 * other + 1))
    held = lax.dynamic_index_in_dim(held, chip, 0, keepdims=False)
    if pair % LANES:
        total = sum((part[:count] for part in got), sums).reshape(count // chips, chips, pair)
        return factor * lax.dot_general(
            jnp.take(total, chip ^ jnp.asarray([0, *others], jnp.int32), axis=1),
            jnp.stack([held] + [part[count:] for part in got]),
            (((1, 2), (0, 2)), ((), ())),
            precision=lax.Precision.HIGHEST,
        )
    vmem = pl.BlockSpec(memory_space=pltpu.VMEM)
    return pl.pallas_call(
        functools.partial(share_kernel, factor, others),
        out_shape=jax.ShapeDtypeStruct((count // chips, cols), jnp.float32),
        in_specs=[vmem] * (2 + len(got)),
        out_specs=vmem,
        scratch_shapes=[pltpu.VMEM((count, pair), jnp.float32)],
    )(*[pltpu.with_memory_space_constraint(array, pltpu.VMEM) for array in (sums, held, *got)])


def solution(mesh):
    placed = (
        P(None, None, ("sec", "blk"), None),
        P(None, ("sec", "blk"), None),
        P(("sec", "blk"), None),
        P(None, None, ("sec", "blk"), None),
        P("blk", None),
        P(),
        P(("sec", "blk")),
    )
    return jax.shard_map(
        shards, mesh=mesh, in_specs=placed, out_specs=P("sec", "blk"), check_vma=False
    )
```

```python
import functools
import math

import jax
import jax.numpy as jnp
import numpy as np
from jax import lax
from jax.experimental import pallas as pl
from jax.experimental.pallas import tpu as pltpu
from jax.sharding import PartitionSpec as P

LANES = 128

GLL_NODES = np.array(
    [
        -1.0,
        -0.8717401485096066,
        -0.5917001814331423,
        -0.2092992179024789,
        0.2092992179024789,
        0.5917001814331423,
        0.8717401485096066,
        1.0,
    ]
)
GLL_WEIGHTS = np.array(
    [
        1.0 / 28.0,
        0.2107042271435061,
        0.3411226924835044,
        0.4124587946587038,
        0.4124587946587038,
        0.3411226924835044,
        0.2107042271435061,
        1.0 / 28.0,
    ]
)


def legendre_seven(nodes):
    before = nodes * 0.0 + 1.0
    current = nodes * 1.0
    for order in range(1, 7):
        following = ((2.0 * order + 1.0) * nodes * current - order * before) / (order + 1.0)
        before = current
        current = following
    return current


def derivative_matrix():
    degree = 7
    values = legendre_seven(GLL_NODES)
    result = np.zeros((8, 8))
    for row_idx in range(8):
        for col_idx in range(8):
            if row_idx != col_idx:
                result[row_idx, col_idx] = values[row_idx] / (
                    values[col_idx] * (GLL_NODES[row_idx] - GLL_NODES[col_idx])
                )
    result[0, 0] = -degree * (degree + 1) / 4.0
    result[7, 7] = degree * (degree + 1) / 4.0
    return result.astype(np.float32)


def point_weights():
    cube = GLL_WEIGHTS[:, None, None] * GLL_WEIGHTS[None, :, None] * GLL_WEIGHTS[None, None, :]
    return cube.reshape(512).astype(np.float32)


def along_tables(points):
    table = derivative_matrix()
    side = table.shape[0]
    lanes = np.arange(LANES)
    per_block = LANES // (side * side)
    i, j, k = lanes // (side * side), lanes // side % side, lanes % side
    along_s = table[j[None, :], j[:, None]] * (i[None, :] == i[:, None]) * (k[None, :] == k[:, None])
    along_t = table[k[None, :], k[:, None]] * (i[None, :] == i[:, None]) * (j[None, :] == j[:, None])
    along_r = [table[p * per_block + i, node] for p in range(points // LANES) for node in range(side)]
    return np.concatenate(
        [along_s, along_t, np.stack(along_r), point_weights().reshape(-1, LANES)], axis=0
    ).astype(np.float32)


def halves_of(values):
    high = values.astype(jnp.bfloat16)
    return high, (values - high.astype(jnp.float32)).astype(jnp.bfloat16)


def pair_rows(rows, height):
    elements = rows.shape[0]
    turn = lax.broadcasted_iota(jnp.int32, (height, LANES), 0) % elements
    spread = jnp.broadcast_to(rows[0:1], (height, LANES))
    for elem in range(1, elements):
        spread = jnp.where(turn == elem, rows[elem : elem + 1], spread)
    return spread


def stored_kernel(
    blocks,
    map_hbm,
    order_hbm,
    velocity_hbm,
    geometry_hbm,
    mass_hbm,
    table_hbm,
    eigvecs_hbm,
    stored_ref,
    send_ref,
    keep_ref,
    map_ref,
    order_ref,
    velocity_ref,
    geometry_ref,
    mass_ref,
    table_ref,
    eigvecs_ref,
    columns_ref,
    semaphores,
):
    fields, components, elements, points = velocity_hbm.shape
    own, mode_count = eigvecs_hbm.shape
    parts = points // LANES
    rows = fields * elements
    chunks = [(c, p) for c in range(components) for p in range(parts)]
    small = [
        (velocity_hbm, velocity_ref),
        (table_hbm, table_ref),
        (geometry_hbm, geometry_ref),
        (mass_hbm, mass_ref),
        (order_hbm, order_ref),
        (eigvecs_hbm, eigvecs_ref),
        (map_hbm, map_ref),
    ]
    copies = [
        pltpu.make_async_copy(source, target, semaphores.at[n])
        for n, (source, target) in enumerate(small)
    ]
    for copy in copies:
        copy.start()
    for copy in copies:
        copy.wait()

    packed = [
        velocity_ref[:, c, :, p * LANES : (p + 1) * LANES].reshape(rows, LANES) for c, p in chunks
    ]
    stacked = jnp.concatenate(packed, axis=0)
    st_high, st_low = halves_of(jnp.concatenate([table_ref[:LANES, :], table_ref[LANES : 2 * LANES, :]], axis=1))
    along_st = jnp.dot(
        jnp.concatenate([stacked, stacked], axis=1),
        jnp.concatenate([st_high, st_low], axis=0),
        preferred_element_type=jnp.float32,
    )
    point_row = table_hbm.shape[0] - parts
    side = (point_row - 2 * LANES) // parts
    lower = lax.broadcasted_iota(jnp.int32, (rows, LANES), 1) < LANES // 2
    along_r = []
    for c in range(components):
        nodes = []
        for p in range(parts):
            here = packed[c * parts + p].astype(jnp.float32)
            other = pltpu.roll(here, LANES // 2, 1)
            nodes += [jnp.where(lower, here, other), jnp.where(lower, other, here)]
        for p in range(parts):
            first = 2 * LANES + p * side
            total = table_ref[first : first + 1, :] * nodes[0]
            for node in range(1, side):
                total += table_ref[first + node : first + node + 1, :] * nodes[node]
            along_r.append(total)

    straight = map_ref[0] == 0
    first_row = lax.broadcasted_iota(jnp.int32, (rows, LANES), 0) % elements == 0
    for p in range(parts):
        lanes = slice(p * LANES, (p + 1) * LANES)
        weight = mass_ref[:, lanes] * table_ref[point_row + p : point_row + p + 1, :]
        factors = [pair_rows(weight * geometry_ref[n, :, lanes], rows) for n in range(9)]

        def gradient(component, coord):
            row = (component * parts + p) * rows
            part = along_st[row : row + rows]
            return (
                factors[coord] * along_r[component * parts + p]
                + factors[3 + coord] * part[:, :LANES]
                + factors[6 + coord] * part[:, LANES:]
            )

        for c in range(components):
            after, last = (c + 1) % 3, (c + 2) % 3
            values = gradient(last, after) - gradient(after, last)
            turned = jnp.where(first_row, pltpu.roll(values, rows - 1, 0), pltpu.roll(values, 1, 0))
            values = jnp.where(straight, values, turned).astype(jnp.bfloat16)
            stored_ref[:, c, :, lanes] = values.reshape(fields, elements, LANES)

    selector = (
        lax.broadcasted_iota(jnp.int32, (mode_count, mode_count), 0) == order_ref[...]
    ).astype(jnp.bfloat16)
    columns_ref[...] = sum(
        jnp.dot(piece, selector, preferred_element_type=jnp.float32) for piece in halves_of(eigvecs_ref[...])
    ).T
    cols, chips = mode_count // blocks, blocks // 2
    block = lax.axis_index("blk")
    core = block & 1
    half = mode_count // 4
    for chip in range(chips):
        kept = jnp.where(chip == block // 2, core, 1 - core)
        keep = columns_ref[pl.ds((2 * chip + kept) * cols, cols), :]
        send = columns_ref[pl.ds((2 * chip + 1 - kept) * cols, cols), :]
        keep_ref[chip * cols : (chip + 1) * cols, :] = keep
        row, lane = chip * cols % half, chip * cols // half * own
        send_ref[row : row + cols, lane : lane + own] = send


def stored_vorticity(velocity, geometry, mass, eigvecs, mode_order, elem_map):
    fields, components, elements, points = velocity.shape
    own, mode_count = eigvecs.shape
    blocks = lax.axis_size("blk")
    table = along_tables(points)
    vmem = pl.BlockSpec(memory_space=pltpu.VMEM)
    return pl.pallas_call(
        functools.partial(stored_kernel, blocks),
        out_shape=(
            pltpu.VMEM(velocity.shape, jnp.bfloat16),
            pltpu.VMEM((mode_count // 4, 2 * own), jnp.float32),
            pltpu.VMEM((mode_count // 2, own), jnp.float32),
        ),
        in_specs=[pl.BlockSpec(memory_space=pltpu.HBM)] * 7,
        out_specs=(vmem,) * 3,
        scratch_shapes=[
            pltpu.SMEM(elem_map.shape, jnp.int32),
            pltpu.VMEM((1, mode_count), jnp.int32),
            pltpu.VMEM(velocity.shape, jnp.bfloat16),
            pltpu.VMEM(geometry.shape, jnp.float32),
            pltpu.VMEM(mass.shape, jnp.float32),
            pltpu.VMEM(table.shape, jnp.float32),
            pltpu.VMEM(eigvecs.shape, jnp.float32),
            pltpu.VMEM((mode_count, own), jnp.float32),
            pltpu.SemaphoreType.DMA((7,)),
        ],
    )(
        *[
            pltpu.with_memory_space_constraint(array, pltpu.HBM)
            for array in (
                elem_map,
                mode_order.reshape(1, mode_count),
                velocity,
                geometry,
                mass,
                jnp.asarray(table),
                eigvecs,
            )
        ]
    )


def exchange(block, ds, db):
    sections, blocks = lax.axis_size("sec"), lax.axis_size("blk")
    pairs = [
        (s * blocks + b, (s ^ ds) * blocks + (b ^ db))
        for s in range(sections)
        for b in range(blocks)
    ]
    return lax.ppermute(block, ("sec", "blk"), pairs)


def share_kernel(factor, others, sums_ref, held_ref, *refs):
    *got_refs, out_ref, total_ref = refs
    count, chips = sums_ref.shape[0], len(others) + 1
    fields = out_ref.shape[0]
    total = sums_ref[...]
    for got_ref in got_refs:
        total += got_ref[:count, :]
    total_ref[...] = total
    chip = lax.axis_index("blk") // 2
    left = [total_ref[pl.ds(chip ^ other, fields, stride=chips), :] for other in (0, *others)]
    right = [held_ref[...]] + [got_ref[count:, :] for got_ref in got_refs]
    out_ref[...] = factor * lax.dot_general(
        jnp.concatenate(left, axis=1),
        jnp.concatenate(right, axis=1),
        (((1,), (1,)), ((), ())),
        precision=lax.Precision.HIGHEST,
        preferred_element_type=jnp.float32,
    )


def shards(velocity, geometry, mass, snapshots, eigvecs, mode_order, elem_map):
    sections, blocks = lax.axis_size("sec"), lax.axis_size("blk")
    section, block = lax.axis_index("sec"), lax.axis_index("blk")
    fields, _, elements, _ = velocity.shape
    own, mode_count = eigvecs.shape
    chips, cols, pair = blocks // 2, mode_count // blocks, 2 * own
    factor = 0.25 / math.sqrt(elements * sections * blocks)

    stored, send, keep = stored_vorticity(velocity, geometry, mass, eigvecs, mode_order, elem_map)
    sums = lax.dot_general(
        stored.reshape(fields, -1),
        snapshots.reshape(snapshots.shape[0], -1),
        (((1,), (1,)), ((), ())),
        preferred_element_type=jnp.float32,
    ).reshape(-1, pair)
    count = fields * chips
    got = exchange(jnp.concatenate([sums, send], axis=0), 0, 1)
    sums = sums + got[:count]
    arrived = jnp.concatenate([got[count:, :own], got[count:, own:]], axis=0)
    second = (block & 1) != 0
    held = jnp.concatenate(
        [jnp.where(second, arrived, keep), jnp.where(second, keep, arrived)], axis=1
    ).reshape(chips, cols, pair)

    count //= sections
    parts = sums.reshape(sections, count, pair)
    sums = lax.dynamic_index_in_dim(parts, section, 0, keepdims=False)
    for other in [n for n in (2,3,1) if n < sections] + list(range(4, sections)):
        part = lax.dynamic_index_in_dim(parts, section ^ other, 0, keepdims=False)
        sums = sums + exchange(part, other, 1)

    others = [n for n in (2,3,1) if n < chips] + list(range(4, chips))
    chip = block // 2
    got = []
    for other in others:
        packet = jnp.concatenate([sums, lax.dynamic_index_in_dim(held, chip ^ other, 0, keepdims=False)], axis=0)
        got.append(exchange(packet, 0, 2 * other + 1))
    held = lax.dynamic_index_in_dim(held, chip, 0, keepdims=False)
    if pair % LANES:
        total = sum((part[:count] for part in got), sums).reshape(count // chips, chips, pair)
        return factor * lax.dot_general(
            jnp.take(total, chip ^ jnp.asarray([0, *others], jnp.int32), axis=1),
            jnp.stack([held] + [part[count:] for part in got]),
            (((1, 2), (0, 2)), ((), ())),
            precision=lax.Precision.HIGHEST,
        )
    vmem = pl.BlockSpec(memory_space=pltpu.VMEM)
    return pl.pallas_call(
        functools.partial(share_kernel, factor, others),
        out_shape=jax.ShapeDtypeStruct((count // chips, cols), jnp.float32),
        in_specs=[vmem] * (2 + len(got)),
        out_specs=vmem,
        scratch_shapes=[pltpu.VMEM((count, pair), jnp.float32)],
    )(*[pltpu.with_memory_space_constraint(array, pltpu.VMEM) for array in (sums, held, *got)])


def solution(mesh):
    placed = (
        P(None, None, ("sec", "blk"), None),
        P(None, ("sec", "blk"), None),
        P(("sec", "blk"), None),
        P(None, None, ("sec", "blk"), None),
        P("blk", None),
        P(),
        P(("sec", "blk")),
    )
    return jax.shard_map(
        shards, mesh=mesh, in_specs=placed, out_specs=P("sec", "blk"), check_vma=False
    )
```

```python
import functools
import math

import jax
import jax.numpy as jnp
import numpy as np
from jax import lax
from jax.experimental import pallas as pl
from jax.experimental.pallas import tpu as pltpu
from jax.sharding import PartitionSpec as P

LANES = 128

GLL_NODES = np.array(
    [
        -1.0,
        -0.8717401485096066,
        -0.5917001814331423,
        -0.2092992179024789,
        0.2092992179024789,
        0.5917001814331423,
        0.8717401485096066,
        1.0,
    ]
)
GLL_WEIGHTS = np.array(
    [
        1.0 / 28.0,
        0.2107042271435061,
        0.3411226924835044,
        0.4124587946587038,
        0.4124587946587038,
        0.3411226924835044,
        0.2107042271435061,
        1.0 / 28.0,
    ]
)


def legendre_seven(nodes):
    before = nodes * 0.0 + 1.0
    current = nodes * 1.0
    for order in range(1, 7):
        following = ((2.0 * order + 1.0) * nodes * current - order * before) / (order + 1.0)
        before = current
        current = following
    return current


def derivative_matrix():
    degree = 7
    values = legendre_seven(GLL_NODES)
    result = np.zeros((8, 8))
    for row_idx in range(8):
        for col_idx in range(8):
            if row_idx != col_idx:
                result[row_idx, col_idx] = values[row_idx] / (
                    values[col_idx] * (GLL_NODES[row_idx] - GLL_NODES[col_idx])
                )
    result[0, 0] = -degree * (degree + 1) / 4.0
    result[7, 7] = degree * (degree + 1) / 4.0
    return result.astype(np.float32)


def point_weights():
    cube = GLL_WEIGHTS[:, None, None] * GLL_WEIGHTS[None, :, None] * GLL_WEIGHTS[None, None, :]
    return cube.reshape(512).astype(np.float32)


def along_tables(points):
    table = derivative_matrix()
    side = table.shape[0]
    lanes = np.arange(LANES)
    per_block = LANES // (side * side)
    i, j, k = lanes // (side * side), lanes // side % side, lanes % side
    along_s = table[j[None, :], j[:, None]] * (i[None, :] == i[:, None]) * (k[None, :] == k[:, None])
    along_t = table[k[None, :], k[:, None]] * (i[None, :] == i[:, None]) * (j[None, :] == j[:, None])
    along_r = [table[p * per_block + i, node] for p in range(points // LANES) for node in range(side)]
    return np.concatenate(
        [along_s, along_t, np.stack(along_r), point_weights().reshape(-1, LANES)], axis=0
    ).astype(np.float32)


def pieces_of(values):
    pieces = []
    for _ in range(3):
        pieces.append(values.astype(jnp.bfloat16))
        values = values - pieces[-1].astype(jnp.float32)
    return pieces


def pair_rows(rows, height):
    elements = rows.shape[0]
    turn = lax.broadcasted_iota(jnp.int32, (height, LANES), 0) % elements
    spread = jnp.broadcast_to(rows[0:1], (height, LANES))
    for elem in range(1, elements):
        spread = jnp.where(turn == elem, rows[elem : elem + 1], spread)
    return spread


def stored_kernel(
    blocks,
    map_hbm,
    order_hbm,
    velocity_hbm,
    geometry_hbm,
    mass_hbm,
    table_hbm,
    eigvecs_hbm,
    stored_ref,
    send_ref,
    keep_ref,
    map_ref,
    order_ref,
    velocity_ref,
    geometry_ref,
    mass_ref,
    table_ref,
    eigvecs_ref,
    columns_ref,
    semaphores,
):
    fields, components, elements, points = velocity_hbm.shape
    own, mode_count = eigvecs_hbm.shape
    parts = points // LANES
    rows = fields * elements
    chunks = [(c, p) for c in range(components) for p in range(parts)]
    small = [
        (velocity_hbm, velocity_ref),
        (table_hbm, table_ref),
        (geometry_hbm, geometry_ref),
        (mass_hbm, mass_ref),
        (order_hbm, order_ref),
        (eigvecs_hbm, eigvecs_ref),
        (map_hbm, map_ref),
    ]
    copies = [
        pltpu.make_async_copy(source, target, semaphores.at[n])
        for n, (source, target) in enumerate(small)
    ]
    for copy in copies:
        copy.start()
    for copy in copies:
        copy.wait()

    packed = [
        velocity_ref[:, c, :, p * LANES : (p + 1) * LANES].reshape(rows, LANES) for c, p in chunks
    ]
    stacked = jnp.concatenate(packed, axis=0)
    st = pieces_of(jnp.concatenate([table_ref[:LANES, :], table_ref[LANES : 2 * LANES, :]], axis=1))
    along_st = jnp.dot(
        jnp.concatenate([stacked] * len(st), axis=1),
        jnp.concatenate(st, axis=0),
        preferred_element_type=jnp.float32,
    )
    point_row = table_hbm.shape[0] - parts
    side = (point_row - 2 * LANES) // parts
    lower = lax.broadcasted_iota(jnp.int32, (rows, LANES), 1) < LANES // 2
    along_r = []
    for c in range(components):
        nodes = []
        for p in range(parts):
            here = packed[c * parts + p].astype(jnp.float32)
            other = pltpu.roll(here, LANES // 2, 1)
            nodes += [jnp.where(lower, here, other), jnp.where(lower, other, here)]
        for p in range(parts):
            first = 2 * LANES + p * side
            total = table_ref[first : first + 1, :] * nodes[0]
            for node in range(1, side):
                total += table_ref[first + node : first + node + 1, :] * nodes[node]
            along_r.append(total)

    straight = map_ref[0] == 0
    first_row = lax.broadcasted_iota(jnp.int32, (rows, LANES), 0) % elements == 0
    for p in range(parts):
        lanes = slice(p * LANES, (p + 1) * LANES)
        weight = mass_ref[:, lanes] * table_ref[point_row + p : point_row + p + 1, :]
        factors = [pair_rows(weight * geometry_ref[n, :, lanes], rows) for n in range(9)]

        def gradient(component, coord):
            row = (component * parts + p) * rows
            part = along_st[row : row + rows]
            return (
                factors[coord] * along_r[component * parts + p]
                + factors[3 + coord] * part[:, :LANES]
                + factors[6 + coord] * part[:, LANES:]
            )

        for c in range(components):
            after, last = (c + 1) % 3, (c + 2) % 3
            values = gradient(last, after) - gradient(after, last)
            turned = jnp.where(first_row, pltpu.roll(values, rows - 1, 0), pltpu.roll(values, 1, 0))
            values = jnp.where(straight, values, turned).astype(jnp.bfloat16)
            stored_ref[:, c, :, lanes] = values.reshape(fields, elements, LANES)

    selector = (
        lax.broadcasted_iota(jnp.int32, (mode_count, mode_count), 0) == order_ref[...]
    ).astype(jnp.bfloat16)
    columns_ref[...] = sum(
        jnp.dot(piece, selector, preferred_element_type=jnp.float32) for piece in pieces_of(eigvecs_ref[...])
    ).T
    cols, chips = mode_count // blocks, blocks // 2
    block = lax.axis_index("blk")
    core = block & 1
    half = mode_count // 4
    for chip in range(chips):
        kept = jnp.where(chip == block // 2, core, 1 - core)
        keep = columns_ref[pl.ds((2 * chip + kept) * cols, cols), :]
        send = columns_ref[pl.ds((2 * chip + 1 - kept) * cols, cols), :]
        keep_ref[chip * cols : (chip + 1) * cols, :] = keep
        row, lane = chip * cols % half, chip * cols // half * own
        send_ref[row : row + cols, lane : lane + own] = send


def stored_vorticity(velocity, geometry, mass, eigvecs, mode_order, elem_map):
    fields, components, elements, points = velocity.shape
    own, mode_count = eigvecs.shape
    blocks = lax.axis_size("blk")
    table = along_tables(points)
    vmem = pl.BlockSpec(memory_space=pltpu.VMEM)
    return pl.pallas_call(
        functools.partial(stored_kernel, blocks),
        out_shape=(
            pltpu.VMEM(velocity.shape, jnp.bfloat16),
            pltpu.VMEM((mode_count // 4, 2 * own), jnp.float32),
            pltpu.VMEM((mode_count // 2, own), jnp.float32),
        ),
        in_specs=[pl.BlockSpec(memory_space=pltpu.HBM)] * 7,
        out_specs=(vmem,) * 3,
        scratch_shapes=[
            pltpu.SMEM(elem_map.shape, jnp.int32),
            pltpu.VMEM((1, mode_count), jnp.int32),
            pltpu.VMEM(velocity.shape, jnp.bfloat16),
            pltpu.VMEM(geometry.shape, jnp.float32),
            pltpu.VMEM(mass.shape, jnp.float32),
            pltpu.VMEM(table.shape, jnp.float32),
            pltpu.VMEM(eigvecs.shape, jnp.float32),
            pltpu.VMEM((mode_count, own), jnp.float32),
            pltpu.SemaphoreType.DMA((7,)),
        ],
    )(
        *[
            pltpu.with_memory_space_constraint(array, pltpu.HBM)
            for array in (
                elem_map,
                mode_order.reshape(1, mode_count),
                velocity,
                geometry,
                mass,
                jnp.asarray(table),
                eigvecs,
            )
        ]
    )


def exchange(block, ds, db):
    sections, blocks = lax.axis_size("sec"), lax.axis_size("blk")
    pairs = [
        (s * blocks + b, (s ^ ds) * blocks + (b ^ db))
        for s in range(sections)
        for b in range(blocks)
    ]
    return lax.ppermute(block, ("sec", "blk"), pairs)


def share_kernel(factor, others, sums_ref, held_ref, *refs):
    *got_refs, out_ref, total_ref = refs
    count, chips = sums_ref.shape[0], len(others) + 1
    fields = out_ref.shape[0]
    total = sums_ref[...]
    for got_ref in got_refs:
        total += got_ref[:count, :]
    total_ref[...] = total
    chip = lax.axis_index("blk") // 2
    left = [total_ref[pl.ds(chip ^ other, fields, stride=chips), :] for other in (0, *others)]
    right = [held_ref[...]] + [got_ref[count:, :] for got_ref in got_refs]
    out_ref[...] = factor * lax.dot_general(
        jnp.concatenate(left, axis=1),
        jnp.concatenate(right, axis=1),
        (((1,), (1,)), ((), ())),
        precision=lax.Precision.HIGHEST,
        preferred_element_type=jnp.float32,
    )


def shards(velocity, geometry, mass, snapshots, eigvecs, mode_order, elem_map):
    sections, blocks = lax.axis_size("sec"), lax.axis_size("blk")
    section, block = lax.axis_index("sec"), lax.axis_index("blk")
    fields, _, elements, _ = velocity.shape
    own, mode_count = eigvecs.shape
    chips, cols, pair = blocks // 2, mode_count // blocks, 2 * own
    factor = 0.25 / math.sqrt(elements * sections * blocks)

    stored, send, keep = stored_vorticity(velocity, geometry, mass, eigvecs, mode_order, elem_map)
    sums = lax.dot_general(
        stored.reshape(fields, -1),
        snapshots.reshape(snapshots.shape[0], -1),
        (((1,), (1,)), ((), ())),
        preferred_element_type=jnp.float32,
    ).reshape(-1, pair)
    count = fields * chips
    got = exchange(jnp.concatenate([sums, send], axis=0), 0, 1)
    sums = sums + got[:count]
    arrived = jnp.concatenate([got[count:, :own], got[count:, own:]], axis=0)
    second = (block & 1) != 0
    held = jnp.concatenate(
        [jnp.where(second, arrived, keep), jnp.where(second, keep, arrived)], axis=1
    ).reshape(chips, cols, pair)

    count //= sections
    parts = sums.reshape(sections, count, pair)
    sums = lax.dynamic_index_in_dim(parts, section, 0, keepdims=False)
    for other in [n for n in (2,3,1) if n < sections] + list(range(4, sections)):
        part = lax.dynamic_index_in_dim(parts, section ^ other, 0, keepdims=False)
        sums = sums + exchange(part, other, 1)

    others = [n for n in (2,3,1) if n < chips] + list(range(4, chips))
    chip = block // 2
    got = []
    for other in others:
        packet = jnp.concatenate([sums, lax.dynamic_index_in_dim(held, chip ^ other, 0, keepdims=False)], axis=0)
        got.append(exchange(packet, 0, 2 * other + 1))
    held = lax.dynamic_index_in_dim(held, chip, 0, keepdims=False)
    if pair % LANES:
        total = sum((part[:count] for part in got), sums).reshape(count // chips, chips, pair)
        return factor * lax.dot_general(
            jnp.take(total, chip ^ jnp.asarray([0, *others], jnp.int32), axis=1),
            jnp.stack([held] + [part[count:] for part in got]),
            (((1, 2), (0, 2)), ((), ())),
            precision=lax.Precision.HIGHEST,
        )
    vmem = pl.BlockSpec(memory_space=pltpu.VMEM)
    return pl.pallas_call(
        functools.partial(share_kernel, factor, others),
        out_shape=jax.ShapeDtypeStruct((count // chips, cols), jnp.float32),
        in_specs=[vmem] * (2 + len(got)),
        out_specs=vmem,
        scratch_shapes=[pltpu.VMEM((count, pair), jnp.float32)],
    )(*[pltpu.with_memory_space_constraint(array, pltpu.VMEM) for array in (sums, held, *got)])


def solution(mesh):
    placed = (
        P(None, None, ("sec", "blk"), None),
        P(None, ("sec", "blk"), None),
        P(("sec", "blk"), None),
        P(None, None, ("sec", "blk"), None),
        P("blk", None),
        P(),
        P(("sec", "blk")),
    )
    return jax.shard_map(
        shards, mesh=mesh, in_specs=placed, out_specs=P("sec", "blk"), check_vma=False
    )
```

```python
import functools
import math

import jax
import jax.numpy as jnp
import numpy as np
from jax import lax
from jax.experimental import pallas as pl
from jax.experimental.pallas import tpu as pltpu
from jax.sharding import PartitionSpec as P

LANES = 128

GLL_NODES = np.array(
    [
        -1.0,
        -0.8717401485096066,
        -0.5917001814331423,
        -0.2092992179024789,
        0.2092992179024789,
        0.5917001814331423,
        0.8717401485096066,
        1.0,
    ]
)
GLL_WEIGHTS = np.array(
    [
        1.0 / 28.0,
        0.2107042271435061,
        0.3411226924835044,
        0.4124587946587038,
        0.4124587946587038,
        0.3411226924835044,
        0.2107042271435061,
        1.0 / 28.0,
    ]
)


def legendre_seven(nodes):
    before = nodes * 0.0 + 1.0
    current = nodes * 1.0
    for order in range(1, 7):
        following = ((2.0 * order + 1.0) * nodes * current - order * before) / (order + 1.0)
        before = current
        current = following
    return current


def derivative_matrix():
    degree = 7
    values = legendre_seven(GLL_NODES)
    result = np.zeros((8, 8))
    for row_idx in range(8):
        for col_idx in range(8):
            if row_idx != col_idx:
                result[row_idx, col_idx] = values[row_idx] / (
                    values[col_idx] * (GLL_NODES[row_idx] - GLL_NODES[col_idx])
                )
    result[0, 0] = -degree * (degree + 1) / 4.0
    result[7, 7] = degree * (degree + 1) / 4.0
    return result.astype(np.float32)


def point_weights():
    cube = GLL_WEIGHTS[:, None, None] * GLL_WEIGHTS[None, :, None] * GLL_WEIGHTS[None, None, :]
    return cube.reshape(512).astype(np.float32)


def along_tables(points):
    table = derivative_matrix()
    side = table.shape[0]
    lanes = np.arange(LANES)
    per_block = LANES // (side * side)
    i, j, k = lanes // (side * side), lanes // side % side, lanes % side
    along_s = table[j[None, :], j[:, None]] * (i[None, :] == i[:, None]) * (k[None, :] == k[:, None])
    along_t = table[k[None, :], k[:, None]] * (i[None, :] == i[:, None]) * (j[None, :] == j[:, None])
    along_r = [table[p * per_block + i, node] for p in range(points // LANES) for node in range(side)]
    return np.concatenate(
        [along_s, along_t, np.stack(along_r), point_weights().reshape(-1, LANES)], axis=0
    ).astype(np.float32)


def pieces_of(values):
    pieces = []
    for _ in range(3):
        pieces.append(values.astype(jnp.bfloat16))
        values = values - pieces[-1].astype(jnp.float32)
    return pieces


def pair_rows(rows, height):
    elements = rows.shape[0]
    turn = lax.broadcasted_iota(jnp.int32, (height, LANES), 0) % elements
    spread = jnp.broadcast_to(rows[0:1], (height, LANES))
    for elem in range(1, elements):
        spread = jnp.where(turn == elem, rows[elem : elem + 1], spread)
    return spread


def stored_kernel(
    blocks,
    map_hbm,
    order_hbm,
    velocity_hbm,
    geometry_hbm,
    mass_hbm,
    table_hbm,
    eigvecs_hbm,
    stored_ref,
    send_ref,
    keep_ref,
    map_ref,
    order_ref,
    velocity_ref,
    geometry_ref,
    mass_ref,
    table_ref,
    eigvecs_ref,
    columns_ref,
    semaphores,
):
    fields, components, elements, points = velocity_hbm.shape
    own, mode_count = eigvecs_hbm.shape
    parts = points // LANES
    rows = fields * elements
    chunks = [(c, p) for c in range(components) for p in range(parts)]
    small = [
        (velocity_hbm, velocity_ref),
        (table_hbm, table_ref),
        (geometry_hbm, geometry_ref),
        (mass_hbm, mass_ref),
        (order_hbm, order_ref),
        (eigvecs_hbm, eigvecs_ref),
        (map_hbm, map_ref),
    ]
    copies = [
        pltpu.make_async_copy(source, target, semaphores.at[n])
        for n, (source, target) in enumerate(small)
    ]
    for copy in copies:
        copy.start()
    for copy in copies:
        copy.wait()

    packed = [
        velocity_ref[:, c, :, p * LANES : (p + 1) * LANES].reshape(rows, LANES) for c, p in chunks
    ]
    stacked = jnp.concatenate(packed, axis=0)
    st = pieces_of(jnp.concatenate([table_ref[:LANES, :], table_ref[LANES : 2 * LANES, :]], axis=1))
    along_st = jnp.dot(
        jnp.concatenate([stacked] * len(st), axis=1),
        jnp.concatenate(st, axis=0),
        preferred_element_type=jnp.float32,
    )
    point_row = table_hbm.shape[0] - parts
    side = (point_row - 2 * LANES) // parts
    lower = lax.broadcasted_iota(jnp.int32, (rows, LANES), 1) < LANES // 2
    along_r = []
    for c in range(components):
        nodes = []
        for p in range(parts):
            here = packed[c * parts + p].astype(jnp.float32)
            other = pltpu.roll(here, LANES // 2, 1)
            nodes += [jnp.where(lower, here, other), jnp.where(lower, other, here)]
        for p in range(parts):
            first = 2 * LANES + p * side
            total = table_ref[first : first + 1, :] * nodes[0]
            for node in range(1, side):
                total += table_ref[first + node : first + node + 1, :] * nodes[node]
            along_r.append(total)

    straight = map_ref[0] == 0
    first_row = lax.broadcasted_iota(jnp.int32, (rows, LANES), 0) % elements == 0
    for p in range(parts):
        lanes = slice(p * LANES, (p + 1) * LANES)
        weight = mass_ref[:, lanes] * table_ref[point_row + p : point_row + p + 1, :]
        factors = [pair_rows(weight * geometry_ref[n, :, lanes], rows) for n in range(9)]

        def gradient(component, coord):
            row = (component * parts + p) * rows
            part = along_st[row : row + rows]
            return (
                factors[coord] * along_r[component * parts + p]
                + factors[3 + coord] * part[:, :LANES]
                + factors[6 + coord] * part[:, LANES:]
            )

        for c in range(components):
            after, last = (c + 1) % 3, (c + 2) % 3
            values = gradient(last, after) - gradient(after, last)
            turned = jnp.where(first_row, pltpu.roll(values, rows - 1, 0), pltpu.roll(values, 1, 0))
            values = jnp.where(straight, values, turned).astype(jnp.bfloat16)
            stored_ref[:, c, :, lanes] = values.reshape(fields, elements, LANES)

    selector = (
        lax.broadcasted_iota(jnp.int32, (mode_count, mode_count), 0) == order_ref[...]
    ).astype(jnp.bfloat16)
    columns_ref[...] = sum(
        jnp.dot(piece, selector, preferred_element_type=jnp.float32) for piece in pieces_of(eigvecs_ref[...])
    ).T
    cols, chips = mode_count // blocks, blocks // 2
    block = lax.axis_index("blk")
    core = block & 1
    half = mode_count // 4
    for chip in range(chips):
        kept = jnp.where(chip == block // 2, core, 1 - core)
        keep = columns_ref[pl.ds((2 * chip + kept) * cols, cols), :]
        send = columns_ref[pl.ds((2 * chip + 1 - kept) * cols, cols), :]
        keep_ref[chip * cols : (chip + 1) * cols, :] = keep
        row, lane = chip * cols % half, chip * cols // half * own
        send_ref[row : row + cols, lane : lane + own] = send


def stored_vorticity(velocity, geometry, mass, eigvecs, mode_order, elem_map):
    fields, components, elements, points = velocity.shape
    own, mode_count = eigvecs.shape
    blocks = lax.axis_size("blk")
    table = along_tables(points)
    vmem = pl.BlockSpec(memory_space=pltpu.VMEM)
    return pl.pallas_call(
        functools.partial(stored_kernel, blocks),
        out_shape=(
            pltpu.VMEM(velocity.shape, jnp.bfloat16),
            pltpu.VMEM((mode_count // 4, 2 * own), jnp.float32),
            pltpu.VMEM((mode_count // 2, own), jnp.float32),
        ),
        in_specs=[pl.BlockSpec(memory_space=pltpu.HBM)] * 7,
        out_specs=(vmem,) * 3,
        scratch_shapes=[
            pltpu.SMEM(elem_map.shape, jnp.int32),
            pltpu.VMEM((1, mode_count), jnp.int32),
            pltpu.VMEM(velocity.shape, jnp.bfloat16),
            pltpu.VMEM(geometry.shape, jnp.float32),
            pltpu.VMEM(mass.shape, jnp.float32),
            pltpu.VMEM(table.shape, jnp.float32),
            pltpu.VMEM(eigvecs.shape, jnp.float32),
            pltpu.VMEM((mode_count, own), jnp.float32),
            pltpu.SemaphoreType.DMA((7,)),
        ],
    )(
        *[
            pltpu.with_memory_space_constraint(array, pltpu.HBM)
            for array in (
                elem_map,
                mode_order.reshape(1, mode_count),
                velocity,
                geometry,
                mass,
                jnp.asarray(table),
                eigvecs,
            )
        ]
    )


def exchange(block, ds, db):
    sections, blocks = lax.axis_size("sec"), lax.axis_size("blk")
    pairs = [
        (s * blocks + b, (s ^ ds) * blocks + (b ^ db))
        for s in range(sections)
        for b in range(blocks)
    ]
    return lax.ppermute(block, ("sec", "blk"), pairs)


def pass_on(block, distance):
    sections, blocks = lax.axis_size("sec"), lax.axis_size("blk")
    pairs = [
        (s * blocks + b, s * blocks + ((b + 2 * distance) % blocks ^ 1))
        for s in range(sections)
        for b in range(blocks)
    ]
    return lax.ppermute(block, ("sec", "blk"), pairs)


def share_kernel(factor, others, sums_ref, held_ref, *refs):
    *got_refs, out_ref, total_ref = refs
    count, chips = sums_ref.shape[0], len(others) + 1
    fields = out_ref.shape[0]
    total = sums_ref[...]
    for got_ref in got_refs:
        total += got_ref[:count, :]
    total_ref[...] = total
    chip = lax.axis_index("blk") // 2
    left = [total_ref[pl.ds((chip + chips - other) % chips, fields, stride=chips), :] for other in (0, *others)]
    right = [held_ref[...]] + [got_ref[count:, :] for got_ref in got_refs]
    out_ref[...] = factor * lax.dot_general(
        jnp.concatenate(left, axis=1),
        jnp.concatenate(right, axis=1),
        (((1,), (1,)), ((), ())),
        precision=lax.Precision.HIGHEST,
        preferred_element_type=jnp.float32,
    )


def shards(velocity, geometry, mass, snapshots, eigvecs, mode_order, elem_map):
    sections, blocks = lax.axis_size("sec"), lax.axis_size("blk")
    section, block = lax.axis_index("sec"), lax.axis_index("blk")
    fields, _, elements, _ = velocity.shape
    own, mode_count = eigvecs.shape
    chips, cols, pair = blocks // 2, mode_count // blocks, 2 * own
    factor = 0.25 / math.sqrt(elements * sections * blocks)

    stored, send, keep = stored_vorticity(velocity, geometry, mass, eigvecs, mode_order, elem_map)
    sums = lax.dot_general(
        stored.reshape(fields, -1),
        snapshots.reshape(snapshots.shape[0], -1),
        (((1,), (1,)), ((), ())),
        preferred_element_type=jnp.float32,
    ).reshape(-1, pair)
    count = fields * chips
    got = exchange(jnp.concatenate([sums, send], axis=0), 0, 1)
    sums = sums + got[:count]
    arrived = jnp.concatenate([got[count:, :own], got[count:, own:]], axis=0)
    second = (block & 1) != 0
    held = jnp.concatenate(
        [jnp.where(second, arrived, keep), jnp.where(second, keep, arrived)], axis=1
    ).reshape(chips, cols, pair)

    count //= sections
    parts = sums.reshape(sections, count, pair)
    sums = lax.dynamic_index_in_dim(parts, section, 0, keepdims=False)
    for other in [n for n in (2,3,1) if n < sections] + list(range(4, sections)):
        part = lax.dynamic_index_in_dim(parts, section ^ other, 0, keepdims=False)
        sums = sums + exchange(part, other, 1)

    others = [n for n in (1,2,3) if n < chips] + list(range(4, chips))
    chip = block // 2
    got = []
    for other in others:
        away = lax.dynamic_index_in_dim(held, (chip + other) % chips, 0, keepdims=False)
        got.append(pass_on(jnp.concatenate([sums, away], axis=0), other))
    held = lax.dynamic_index_in_dim(held, chip, 0, keepdims=False)
    if pair % LANES:
        total = sum((part[:count] for part in got), sums).reshape(count // chips, chips, pair)
        return factor * lax.dot_general(
            jnp.take(total, (chip - jnp.asarray([0, *others], jnp.int32)) % chips, axis=1),
            jnp.stack([held] + [part[count:] for part in got]),
            (((1, 2), (0, 2)), ((), ())),
            precision=lax.Precision.HIGHEST,
        )
    vmem = pl.BlockSpec(memory_space=pltpu.VMEM)
    return pl.pallas_call(
        functools.partial(share_kernel, factor, others),
        out_shape=jax.ShapeDtypeStruct((count // chips, cols), jnp.float32),
        in_specs=[vmem] * (2 + len(got)),
        out_specs=vmem,
        scratch_shapes=[pltpu.VMEM((count, pair), jnp.float32)],
    )(*[pltpu.with_memory_space_constraint(array, pltpu.VMEM) for array in (sums, held, *got)])


def solution(mesh):
    placed = (
        P(None, None, ("sec", "blk"), None),
        P(None, ("sec", "blk"), None),
        P(("sec", "blk"), None),
        P(None, None, ("sec", "blk"), None),
        P("blk", None),
        P(),
        P(("sec", "blk")),
    )
    return jax.shard_map(
        shards, mesh=mesh, in_specs=placed, out_specs=P("sec", "blk"), check_vma=False
    )
```

```python
import functools
import math

import jax
import jax.numpy as jnp
import numpy as np
from jax import lax
from jax.experimental import pallas as pl
from jax.experimental.pallas import tpu as pltpu
from jax.sharding import PartitionSpec as P

LANES = 128

GLL_NODES = np.array(
    [
        -1.0,
        -0.8717401485096066,
        -0.5917001814331423,
        -0.2092992179024789,
        0.2092992179024789,
        0.5917001814331423,
        0.8717401485096066,
        1.0,
    ]
)
GLL_WEIGHTS = np.array(
    [
        1.0 / 28.0,
        0.2107042271435061,
        0.3411226924835044,
        0.4124587946587038,
        0.4124587946587038,
        0.3411226924835044,
        0.2107042271435061,
        1.0 / 28.0,
    ]
)


def legendre_seven(nodes):
    before = nodes * 0.0 + 1.0
    current = nodes * 1.0
    for order in range(1, 7):
        following = ((2.0 * order + 1.0) * nodes * current - order * before) / (order + 1.0)
        before = current
        current = following
    return current


def derivative_matrix():
    degree = 7
    values = legendre_seven(GLL_NODES)
    result = np.zeros((8, 8))
    for row_idx in range(8):
        for col_idx in range(8):
            if row_idx != col_idx:
                result[row_idx, col_idx] = values[row_idx] / (
                    values[col_idx] * (GLL_NODES[row_idx] - GLL_NODES[col_idx])
                )
    result[0, 0] = -degree * (degree + 1) / 4.0
    result[7, 7] = degree * (degree + 1) / 4.0
    return result.astype(np.float32)


def point_weights():
    cube = GLL_WEIGHTS[:, None, None] * GLL_WEIGHTS[None, :, None] * GLL_WEIGHTS[None, None, :]
    return cube.reshape(512).astype(np.float32)


def along_tables(points):
    table = derivative_matrix()
    side = table.shape[0]
    lanes = np.arange(LANES)
    per_block = LANES // (side * side)
    i, j, k = lanes // (side * side), lanes // side % side, lanes % side
    along_s = table[j[None, :], j[:, None]] * (i[None, :] == i[:, None]) * (k[None, :] == k[:, None])
    along_t = table[k[None, :], k[:, None]] * (i[None, :] == i[:, None]) * (j[None, :] == j[:, None])
    along_r = [table[p * per_block + i, node] for p in range(points // LANES) for node in range(side)]
    return np.concatenate(
        [along_s, along_t, np.stack(along_r), point_weights().reshape(-1, LANES)], axis=0
    ).astype(np.float32)


def pieces_of(values):
    pieces = []
    for _ in range(3):
        pieces.append(values.astype(jnp.bfloat16))
        values = values - pieces[-1].astype(jnp.float32)
    return pieces


def pair_rows(rows, height):
    elements = rows.shape[0]
    turn = lax.broadcasted_iota(jnp.int32, (height, LANES), 0) % elements
    spread = jnp.broadcast_to(rows[0:1], (height, LANES))
    for elem in range(1, elements):
        spread = jnp.where(turn == elem, rows[elem : elem + 1], spread)
    return spread


def stored_kernel(
    blocks,
    map_hbm,
    order_hbm,
    velocity_hbm,
    geometry_hbm,
    mass_hbm,
    table_hbm,
    eigvecs_hbm,
    stored_ref,
    send_ref,
    keep_ref,
    map_ref,
    order_ref,
    velocity_ref,
    geometry_ref,
    mass_ref,
    table_ref,
    eigvecs_ref,
    columns_ref,
    semaphores,
):
    fields, components, elements, points = velocity_hbm.shape
    own, mode_count = eigvecs_hbm.shape
    parts = points // LANES
    rows = fields * elements
    chunks = [(c, p) for c in range(components) for p in range(parts)]
    small = [
        (velocity_hbm, velocity_ref),
        (table_hbm, table_ref),
        (geometry_hbm, geometry_ref),
        (mass_hbm, mass_ref),
        (order_hbm, order_ref),
        (eigvecs_hbm, eigvecs_ref),
        (map_hbm, map_ref),
    ]
    copies = [
        pltpu.make_async_copy(source, target, semaphores.at[n])
        for n, (source, target) in enumerate(small)
    ]
    for copy in copies:
        copy.start()
    for copy in copies:
        copy.wait()

    packed = [
        velocity_ref[:, c, :, p * LANES : (p + 1) * LANES].reshape(rows, LANES) for c, p in chunks
    ]
    stacked = jnp.concatenate(packed, axis=0)
    st = pieces_of(jnp.concatenate([table_ref[:LANES, :], table_ref[LANES : 2 * LANES, :]], axis=1))
    along_st = jnp.dot(
        jnp.concatenate([stacked] * len(st), axis=1),
        jnp.concatenate(st, axis=0),
        preferred_element_type=jnp.float32,
    )
    point_row = table_hbm.shape[0] - parts
    side = (point_row - 2 * LANES) // parts
    lower = lax.broadcasted_iota(jnp.int32, (rows, LANES), 1) < LANES // 2
    along_r = []
    for c in range(components):
        nodes = []
        for p in range(parts):
            here = packed[c * parts + p].astype(jnp.float32)
            other = pltpu.roll(here, LANES // 2, 1)
            nodes += [jnp.where(lower, here, other), jnp.where(lower, other, here)]
        for p in range(parts):
            first = 2 * LANES + p * side
            total = table_ref[first : first + 1, :] * nodes[0]
            for node in range(1, side):
                total += table_ref[first + node : first + node + 1, :] * nodes[node]
            along_r.append(total)

    straight = map_ref[0] == 0
    first_row = lax.broadcasted_iota(jnp.int32, (rows, LANES), 0) % elements == 0
    for p in range(parts):
        lanes = slice(p * LANES, (p + 1) * LANES)
        weight = mass_ref[:, lanes] * table_ref[point_row + p : point_row + p + 1, :]
        factors = [pair_rows(weight * geometry_ref[n, :, lanes], rows) for n in range(9)]

        def gradient(component, coord):
            row = (component * parts + p) * rows
            part = along_st[row : row + rows]
            return (
                factors[coord] * along_r[component * parts + p]
                + factors[3 + coord] * part[:, :LANES]
                + factors[6 + coord] * part[:, LANES:]
            )

        for c in range(components):
            after, last = (c + 1) % 3, (c + 2) % 3
            values = gradient(last, after) - gradient(after, last)
            turned = jnp.where(first_row, pltpu.roll(values, rows - 1, 0), pltpu.roll(values, 1, 0))
            values = jnp.where(straight, values, turned).astype(jnp.bfloat16)
            stored_ref[:, c, :, lanes] = values.reshape(fields, elements, LANES)

    selector = (
        lax.broadcasted_iota(jnp.int32, (mode_count, mode_count), 0) == order_ref[...]
    ).astype(jnp.bfloat16)
    columns_ref[...] = sum(
        jnp.dot(piece, selector, preferred_element_type=jnp.float32) for piece in pieces_of(eigvecs_ref[...])
    ).T
    cols, chips = mode_count // blocks, blocks // 2
    block = lax.axis_index("blk")
    core = block & 1
    half = mode_count // 4
    for chip in range(chips):
        kept = jnp.where(chip == block // 2, core, 1 - core)
        keep = columns_ref[pl.ds((2 * chip + kept) * cols, cols), :]
        send = columns_ref[pl.ds((2 * chip + 1 - kept) * cols, cols), :]
        keep_ref[chip * cols : (chip + 1) * cols, :] = keep
        row, lane = chip * cols % half, chip * cols // half * own
        send_ref[row : row + cols, lane : lane + own] = send


def stored_vorticity(velocity, geometry, mass, eigvecs, mode_order, elem_map):
    fields, components, elements, points = velocity.shape
    own, mode_count = eigvecs.shape
    blocks = lax.axis_size("blk")
    table = along_tables(points)
    vmem = pl.BlockSpec(memory_space=pltpu.VMEM)
    return pl.pallas_call(
        functools.partial(stored_kernel, blocks),
        out_shape=(
            pltpu.VMEM(velocity.shape, jnp.bfloat16),
            pltpu.VMEM((mode_count // 4, 2 * own), jnp.float32),
            pltpu.VMEM((mode_count // 2, own), jnp.float32),
        ),
        in_specs=[pl.BlockSpec(memory_space=pltpu.HBM)] * 7,
        out_specs=(vmem,) * 3,
        scratch_shapes=[
            pltpu.SMEM(elem_map.shape, jnp.int32),
            pltpu.VMEM((1, mode_count), jnp.int32),
            pltpu.VMEM(velocity.shape, jnp.bfloat16),
            pltpu.VMEM(geometry.shape, jnp.float32),
            pltpu.VMEM(mass.shape, jnp.float32),
            pltpu.VMEM(table.shape, jnp.float32),
            pltpu.VMEM(eigvecs.shape, jnp.float32),
            pltpu.VMEM((mode_count, own), jnp.float32),
            pltpu.SemaphoreType.DMA((7,)),
        ],
    )(
        *[
            pltpu.with_memory_space_constraint(array, pltpu.HBM)
            for array in (
                elem_map,
                mode_order.reshape(1, mode_count),
                velocity,
                geometry,
                mass,
                jnp.asarray(table),
                eigvecs,
            )
        ]
    )


def exchange(block, ds, db):
    sections, blocks = lax.axis_size("sec"), lax.axis_size("blk")
    pairs = [
        (s * blocks + b, (s ^ ds) * blocks + (b ^ db))
        for s in range(sections)
        for b in range(blocks)
    ]
    return lax.ppermute(block, ("sec", "blk"), pairs)


def ring_place(section, sections):
    place, shift = section, 1
    while shift < sections:
        place = place ^ (section >> shift)
        shift += 1
    return place


def pass_round(part, distance):
    sections, blocks = lax.axis_size("sec"), lax.axis_size("blk")
    ring = [n ^ (n >> 1) for n in range(sections)]
    pairs = [
        (ring[n] * blocks + b, ring[(n + distance) % sections] * blocks + (b ^ 1))
        for n in range(sections)
        for b in range(blocks)
    ]
    return lax.ppermute(part, ("sec", "blk"), pairs)


def pass_on(block, distance):
    sections, blocks = lax.axis_size("sec"), lax.axis_size("blk")
    pairs = [
        (s * blocks + b, s * blocks + ((b + 2 * distance) % blocks ^ 1))
        for s in range(sections)
        for b in range(blocks)
    ]
    return lax.ppermute(block, ("sec", "blk"), pairs)


def share_kernel(factor, others, sums_ref, held_ref, *refs):
    *got_refs, out_ref, total_ref = refs
    count, chips = sums_ref.shape[0], len(others) + 1
    fields = out_ref.shape[0]
    total = sums_ref[...]
    for got_ref in got_refs:
        total += got_ref[:count, :]
    total_ref[...] = total
    chip = lax.axis_index("blk") // 2
    left = [total_ref[pl.ds((chip + chips - other) % chips, fields, stride=chips), :] for other in (0, *others)]
    right = [held_ref[...]] + [got_ref[count:, :] for got_ref in got_refs]
    out_ref[...] = factor * lax.dot_general(
        jnp.concatenate(left, axis=1),
        jnp.concatenate(right, axis=1),
        (((1,), (1,)), ((), ())),
        precision=lax.Precision.HIGHEST,
        preferred_element_type=jnp.float32,
    )


def shards(velocity, geometry, mass, snapshots, eigvecs, mode_order, elem_map):
    sections, blocks = lax.axis_size("sec"), lax.axis_size("blk")
    section, block = lax.axis_index("sec"), lax.axis_index("blk")
    fields, _, elements, _ = velocity.shape
    own, mode_count = eigvecs.shape
    chips, cols, pair = blocks // 2, mode_count // blocks, 2 * own
    factor = 0.25 / math.sqrt(elements * sections * blocks)

    stored, send, keep = stored_vorticity(velocity, geometry, mass, eigvecs, mode_order, elem_map)
    sums = lax.dot_general(
        stored.reshape(fields, -1),
        snapshots.reshape(snapshots.shape[0], -1),
        (((1,), (1,)), ((), ())),
        preferred_element_type=jnp.float32,
    ).reshape(-1, pair)
    count = fields * chips
    got = exchange(jnp.concatenate([sums, send], axis=0), 0, 1)
    sums = sums + got[:count]
    arrived = jnp.concatenate([got[count:, :own], got[count:, own:]], axis=0)
    second = (block & 1) != 0
    held = jnp.concatenate(
        [jnp.where(second, arrived, keep), jnp.where(second, keep, arrived)], axis=1
    ).reshape(chips, cols, pair)

    count //= sections
    parts = sums.reshape(sections, count, pair)
    sums = lax.dynamic_index_in_dim(parts, section, 0, keepdims=False)
    place = ring_place(section, sections)
    for other in [n for n in (2,1,3) if n < sections] + list(range(4, sections)):
        target = (place + other) % sections
        part = lax.dynamic_index_in_dim(parts, target ^ (target >> 1), 0, keepdims=False)
        sums = sums + pass_round(part, other)

    others = [n for n in (1,2,3) if n < chips] + list(range(4, chips))
    chip = block // 2
    got = []
    for other in others:
        away = lax.dynamic_index_in_dim(held, (chip + other) % chips, 0, keepdims=False)
        got.append(pass_on(jnp.concatenate([sums, away], axis=0), other))
    held = lax.dynamic_index_in_dim(held, chip, 0, keepdims=False)
    if pair % LANES:
        total = sum((part[:count] for part in got), sums).reshape(count // chips, chips, pair)
        return factor * lax.dot_general(
            jnp.take(total, (chip - jnp.asarray([0, *others], jnp.int32)) % chips, axis=1),
            jnp.stack([held] + [part[count:] for part in got]),
            (((1, 2), (0, 2)), ((), ())),
            precision=lax.Precision.HIGHEST,
        )
    vmem = pl.BlockSpec(memory_space=pltpu.VMEM)
    return pl.pallas_call(
        functools.partial(share_kernel, factor, others),
        out_shape=jax.ShapeDtypeStruct((count // chips, cols), jnp.float32),
        in_specs=[vmem] * (2 + len(got)),
        out_specs=vmem,
        scratch_shapes=[pltpu.VMEM((count, pair), jnp.float32)],
    )(*[pltpu.with_memory_space_constraint(array, pltpu.VMEM) for array in (sums, held, *got)])


def solution(mesh):
    placed = (
        P(None, None, ("sec", "blk"), None),
        P(None, ("sec", "blk"), None),
        P(("sec", "blk"), None),
        P(None, None, ("sec", "blk"), None),
        P("blk", None),
        P(),
        P(("sec", "blk")),
    )
    return jax.shard_map(
        shards, mesh=mesh, in_specs=placed, out_specs=P("sec", "blk"), check_vma=False
    )
```

```python
import functools
import math

import jax
import jax.numpy as jnp
import numpy as np
from jax import lax
from jax.experimental import pallas as pl
from jax.experimental.pallas import tpu as pltpu
from jax.sharding import PartitionSpec as P

LANES = 128

GLL_NODES = np.array(
    [
        -1.0,
        -0.8717401485096066,
        -0.5917001814331423,
        -0.2092992179024789,
        0.2092992179024789,
        0.5917001814331423,
        0.8717401485096066,
        1.0,
    ]
)
GLL_WEIGHTS = np.array(
    [
        1.0 / 28.0,
        0.2107042271435061,
        0.3411226924835044,
        0.4124587946587038,
        0.4124587946587038,
        0.3411226924835044,
        0.2107042271435061,
        1.0 / 28.0,
    ]
)


def legendre_seven(nodes):
    before = nodes * 0.0 + 1.0
    current = nodes * 1.0
    for order in range(1, 7):
        following = ((2.0 * order + 1.0) * nodes * current - order * before) / (order + 1.0)
        before = current
        current = following
    return current


def derivative_matrix():
    degree = 7
    values = legendre_seven(GLL_NODES)
    result = np.zeros((8, 8))
    for row_idx in range(8):
        for col_idx in range(8):
            if row_idx != col_idx:
                result[row_idx, col_idx] = values[row_idx] / (
                    values[col_idx] * (GLL_NODES[row_idx] - GLL_NODES[col_idx])
                )
    result[0, 0] = -degree * (degree + 1) / 4.0
    result[7, 7] = degree * (degree + 1) / 4.0
    return result.astype(np.float32)


def point_weights():
    cube = GLL_WEIGHTS[:, None, None] * GLL_WEIGHTS[None, :, None] * GLL_WEIGHTS[None, None, :]
    return cube.reshape(512).astype(np.float32)


def along_tables(points):
    table = derivative_matrix()
    side = table.shape[0]
    lanes = np.arange(LANES)
    per_block = LANES // (side * side)
    i, j, k = lanes // (side * side), lanes // side % side, lanes % side
    along_s = table[j[None, :], j[:, None]] * (i[None, :] == i[:, None]) * (k[None, :] == k[:, None])
    along_t = table[k[None, :], k[:, None]] * (i[None, :] == i[:, None]) * (j[None, :] == j[:, None])
    along_r = [table[p * per_block + i, node] for p in range(points // LANES) for node in range(side)]
    return np.concatenate(
        [along_s, along_t, np.stack(along_r), point_weights().reshape(-1, LANES)], axis=0
    ).astype(np.float32)


def pieces_of(values):
    pieces = []
    for _ in range(3):
        pieces.append(values.astype(jnp.bfloat16))
        values = values - pieces[-1].astype(jnp.float32)
    return pieces


def pair_rows(rows, height):
    elements = rows.shape[0]
    turn = lax.broadcasted_iota(jnp.int32, (height, LANES), 0) % elements
    spread = jnp.broadcast_to(rows[0:1], (height, LANES))
    for elem in range(1, elements):
        spread = jnp.where(turn == elem, rows[elem : elem + 1], spread)
    return spread


def stored_kernel(
    blocks,
    map_hbm,
    order_hbm,
    velocity_hbm,
    geometry_hbm,
    mass_hbm,
    table_hbm,
    eigvecs_hbm,
    stored_ref,
    send_ref,
    keep_ref,
    map_ref,
    order_ref,
    velocity_ref,
    geometry_ref,
    mass_ref,
    table_ref,
    eigvecs_ref,
    columns_ref,
    semaphores,
):
    fields, components, elements, points = velocity_hbm.shape
    own, mode_count = eigvecs_hbm.shape
    parts = points // LANES
    rows = fields * elements
    chunks = [(c, p) for c in range(components) for p in range(parts)]
    small = [
        (velocity_hbm, velocity_ref),
        (table_hbm, table_ref),
        (geometry_hbm, geometry_ref),
        (mass_hbm, mass_ref),
        (order_hbm, order_ref),
        (eigvecs_hbm, eigvecs_ref),
        (map_hbm, map_ref),
    ]
    copies = [
        pltpu.make_async_copy(source, target, semaphores.at[n])
        for n, (source, target) in enumerate(small)
    ]
    for copy in copies:
        copy.start()
    for copy in copies:
        copy.wait()

    packed = [
        velocity_ref[:, c, :, p * LANES : (p + 1) * LANES].reshape(rows, LANES) for c, p in chunks
    ]
    stacked = jnp.concatenate(packed, axis=0)
    st = pieces_of(jnp.concatenate([table_ref[:LANES, :], table_ref[LANES : 2 * LANES, :]], axis=1))
    along_st = jnp.dot(
        jnp.concatenate([stacked] * len(st), axis=1),
        jnp.concatenate(st, axis=0),
        preferred_element_type=jnp.float32,
    )
    point_row = table_hbm.shape[0] - parts
    side = (point_row - 2 * LANES) // parts
    lower = lax.broadcasted_iota(jnp.int32, (rows, LANES), 1) < LANES // 2
    along_r = []
    for c in range(components):
        nodes = []
        for p in range(parts):
            here = packed[c * parts + p].astype(jnp.float32)
            other = pltpu.roll(here, LANES // 2, 1)
            nodes += [jnp.where(lower, here, other), jnp.where(lower, other, here)]
        for p in range(parts):
            first = 2 * LANES + p * side
            total = table_ref[first : first + 1, :] * nodes[0]
            for node in range(1, side):
                total += table_ref[first + node : first + node + 1, :] * nodes[node]
            along_r.append(total)

    straight = map_ref[0] == 0
    first_row = lax.broadcasted_iota(jnp.int32, (rows, LANES), 0) % elements == 0
    for p in range(parts):
        lanes = slice(p * LANES, (p + 1) * LANES)
        weight = mass_ref[:, lanes] * table_ref[point_row + p : point_row + p + 1, :]
        factors = [pair_rows(weight * geometry_ref[n, :, lanes], rows) for n in range(9)]

        def gradient(component, coord):
            row = (component * parts + p) * rows
            part = along_st[row : row + rows]
            return (
                factors[coord] * along_r[component * parts + p]
                + factors[3 + coord] * part[:, :LANES]
                + factors[6 + coord] * part[:, LANES:]
            )

        for c in range(components):
            after, last = (c + 1) % 3, (c + 2) % 3
            values = gradient(last, after) - gradient(after, last)
            turned = jnp.where(first_row, pltpu.roll(values, rows - 1, 0), pltpu.roll(values, 1, 0))
            values = jnp.where(straight, values, turned).astype(jnp.bfloat16)
            stored_ref[:, c, :, lanes] = values.reshape(fields, elements, LANES)

    selector = (
        lax.broadcasted_iota(jnp.int32, (mode_count, mode_count), 0) == order_ref[...]
    ).astype(jnp.bfloat16)
    columns_ref[...] = sum(
        jnp.dot(piece, selector, preferred_element_type=jnp.float32) for piece in pieces_of(eigvecs_ref[...])
    ).T
    cols, chips = mode_count // blocks, blocks // 2
    block = lax.axis_index("blk")
    core = block & 1
    half = mode_count // 4
    for chip in range(chips):
        kept = jnp.where(chip == block // 2, core, 1 - core)
        keep = columns_ref[pl.ds((2 * chip + kept) * cols, cols), :]
        send = columns_ref[pl.ds((2 * chip + 1 - kept) * cols, cols), :]
        keep_ref[chip * cols : (chip + 1) * cols, :] = keep
        row, lane = chip * cols % half, chip * cols // half * own
        send_ref[row : row + cols, lane : lane + own] = send


def stored_vorticity(velocity, geometry, mass, eigvecs, mode_order, elem_map):
    fields, components, elements, points = velocity.shape
    own, mode_count = eigvecs.shape
    blocks = lax.axis_size("blk")
    table = along_tables(points)
    vmem = pl.BlockSpec(memory_space=pltpu.VMEM)
    return pl.pallas_call(
        functools.partial(stored_kernel, blocks),
        out_shape=(
            pltpu.VMEM(velocity.shape, jnp.bfloat16),
            pltpu.VMEM((mode_count // 4, 2 * own), jnp.float32),
            pltpu.VMEM((mode_count // 2, own), jnp.float32),
        ),
        in_specs=[pl.BlockSpec(memory_space=pltpu.HBM)] * 7,
        out_specs=(vmem,) * 3,
        scratch_shapes=[
            pltpu.SMEM(elem_map.shape, jnp.int32),
            pltpu.VMEM((1, mode_count), jnp.int32),
            pltpu.VMEM(velocity.shape, jnp.bfloat16),
            pltpu.VMEM(geometry.shape, jnp.float32),
            pltpu.VMEM(mass.shape, jnp.float32),
            pltpu.VMEM(table.shape, jnp.float32),
            pltpu.VMEM(eigvecs.shape, jnp.float32),
            pltpu.VMEM((mode_count, own), jnp.float32),
            pltpu.SemaphoreType.DMA((7,)),
        ],
    )(
        *[
            pltpu.with_memory_space_constraint(array, pltpu.HBM)
            for array in (
                elem_map,
                mode_order.reshape(1, mode_count),
                velocity,
                geometry,
                mass,
                jnp.asarray(table),
                eigvecs,
            )
        ]
    )


def exchange(block, ds, db):
    sections, blocks = lax.axis_size("sec"), lax.axis_size("blk")
    pairs = [
        (s * blocks + b, (s ^ ds) * blocks + (b ^ db))
        for s in range(sections)
        for b in range(blocks)
    ]
    return lax.ppermute(block, ("sec", "blk"), pairs)


def ring_place(section, sections):
    place, shift = section, 1
    while shift < sections:
        place = place ^ (section >> shift)
        shift += 1
    return place


def pass_round(part, distance):
    sections, blocks = lax.axis_size("sec"), lax.axis_size("blk")
    ring = [n ^ (n >> 1) for n in range(sections)]
    pairs = [
        (ring[n] * blocks + b, ring[(n + distance) % sections] * blocks + (b ^ 1))
        for n in range(sections)
        for b in range(blocks)
    ]
    return lax.ppermute(part, ("sec", "blk"), pairs)


def pass_on(block, distance):
    sections, blocks = lax.axis_size("sec"), lax.axis_size("blk")
    pairs = [
        (s * blocks + b, s * blocks + ((b + 2 * distance) % blocks ^ 1))
        for s in range(sections)
        for b in range(blocks)
    ]
    return lax.ppermute(block, ("sec", "blk"), pairs)


def share_kernel(factor, others, sums_ref, held_ref, *refs):
    *got_refs, out_ref, total_ref = refs
    count, chips = sums_ref.shape[0], len(others) + 1
    fields = out_ref.shape[0]
    total = sums_ref[...]
    for got_ref in got_refs:
        total += got_ref[:count, :]
    total_ref[...] = total
    chip = lax.axis_index("blk") // 2
    left = [total_ref[pl.ds((chip + chips - other) % chips, fields, stride=chips), :] for other in (0, *others)]
    right = [held_ref[...]] + [got_ref[count:, :] for got_ref in got_refs]
    left = pieces_of(jnp.concatenate(left, axis=1))
    right = pieces_of(jnp.concatenate(right, axis=1))
    out_ref[...] = factor * sum(
        lax.dot_general(left[i], right[j], (((1,), (1,)), ((), ())), preferred_element_type=jnp.float32)
        for i, j in ((1, 0), (0, 1), (0, 0))
    )


def shards(velocity, geometry, mass, snapshots, eigvecs, mode_order, elem_map):
    sections, blocks = lax.axis_size("sec"), lax.axis_size("blk")
    section, block = lax.axis_index("sec"), lax.axis_index("blk")
    fields, _, elements, _ = velocity.shape
    own, mode_count = eigvecs.shape
    chips, cols, pair = blocks // 2, mode_count // blocks, 2 * own
    factor = 0.25 / math.sqrt(elements * sections * blocks)

    stored, send, keep = stored_vorticity(velocity, geometry, mass, eigvecs, mode_order, elem_map)
    sums = lax.dot_general(
        stored.reshape(fields, -1),
        snapshots.reshape(snapshots.shape[0], -1),
        (((1,), (1,)), ((), ())),
        preferred_element_type=jnp.float32,
    ).reshape(-1, pair)
    count = fields * chips
    got = exchange(jnp.concatenate([sums, send], axis=0), 0, 1)
    sums = sums + got[:count]
    arrived = jnp.concatenate([got[count:, :own], got[count:, own:]], axis=0)
    second = (block & 1) != 0
    held = jnp.concatenate(
        [jnp.where(second, arrived, keep), jnp.where(second, keep, arrived)], axis=1
    ).reshape(chips, cols, pair)

    count //= sections
    parts = sums.reshape(sections, count, pair)
    sums = lax.dynamic_index_in_dim(parts, section, 0, keepdims=False)
    place = ring_place(section, sections)
    for other in [n for n in (2,1,3) if n < sections] + list(range(4, sections)):
        target = (place + other) % sections
        part = lax.dynamic_index_in_dim(parts, target ^ (target >> 1), 0, keepdims=False)
        sums = sums + pass_round(part, other)

    others = [n for n in (1,2,3) if n < chips] + list(range(4, chips))
    chip = block // 2
    got = []
    for other in others:
        away = lax.dynamic_index_in_dim(held, (chip + other) % chips, 0, keepdims=False)
        got.append(pass_on(jnp.concatenate([sums, away], axis=0), other))
    held = lax.dynamic_index_in_dim(held, chip, 0, keepdims=False)
    if pair % LANES:
        total = sum((part[:count] for part in got), sums).reshape(count // chips, chips, pair)
        return factor * lax.dot_general(
            jnp.take(total, (chip - jnp.asarray([0, *others], jnp.int32)) % chips, axis=1),
            jnp.stack([held] + [part[count:] for part in got]),
            (((1, 2), (0, 2)), ((), ())),
            precision=lax.Precision.HIGHEST,
        )
    vmem = pl.BlockSpec(memory_space=pltpu.VMEM)
    return pl.pallas_call(
        functools.partial(share_kernel, factor, others),
        out_shape=jax.ShapeDtypeStruct((count // chips, cols), jnp.float32),
        in_specs=[vmem] * (2 + len(got)),
        out_specs=vmem,
        scratch_shapes=[pltpu.VMEM((count, pair), jnp.float32)],
    )(*[pltpu.with_memory_space_constraint(array, pltpu.VMEM) for array in (sums, held, *got)])


def solution(mesh):
    placed = (
        P(None, None, ("sec", "blk"), None),
        P(None, ("sec", "blk"), None),
        P(("sec", "blk"), None),
        P(None, None, ("sec", "blk"), None),
        P("blk", None),
        P(),
        P(("sec", "blk")),
    )
    return jax.shard_map(
        shards, mesh=mesh, in_specs=placed, out_specs=P("sec", "blk"), check_vma=False
    )
```
